128 devices in a mesh: blk: 32 (over x, z, y_hi), inner: 4 (over y_lo, core).
Axes of the slice: x: 4, y: 4 (y_hi: 2, y_lo: 2; y = y_hi * 2 + y_lo), z: 4, core: 2. Of those that a mesh axis runs over, the one named last changes fastest.
Arguments:
- image: bfloat16 [12288, 1024], P('blk'), may hold values from -6 to 6
- text: bfloat16 [12288, 1024], P(('blk', 'inner')), may hold values from -1 to 1
- logit_scale: float32 [1], replicated, may hold values from 20 to 50
Outputs:
- loss: float32 [1], replicated
- grad_image: bfloat16 [12288, 1024], P(('blk', 'inner'))
- grad_text: bfloat16 [12288, 1024], P(('blk', 'inner'))
The draws below stay inside these ranges and needn't reach their ends.
All inputs are finite; a program needn't handle non-finite values.
Results may differ from the reference program's by a relative error of at most 0.0044.
Values may be sent and summed in bfloat16 or wider, within the bound.
No kernel may reach another device: no remote copies, remote signals or barrier semaphores. Data moves between devices by JAX's collectives and lax.ppermute only.
A program may use at most 128 MiB of HBM per device.

```python
import math
import jax
import jax.numpy as jnp
from jax import lax

E = 1024
B = 12288


def shared_parts(key):
    keys = jax.random.split(key, 4)
    base = jnp.clip(jax.random.normal(keys[0], (B, E), jnp.float32), -5.0, 5.0)
    noise = jnp.clip(jax.random.normal(keys[1], (B, E), jnp.float32), -5.0, 5.0)
    ramp = 0.5 + jnp.arange(B, dtype=jnp.float32) / B
    row_scale = jnp.exp(jax.random.uniform(keys[2], (B, 1), jnp.float32, math.log(0.4), math.log(2.5))) * ramp[:, None]
    col_scale = jnp.exp(jax.random.uniform(keys[3], (B, 1), jnp.float32, math.log(0.4), math.log(2.5)))
    return (base, noise, row_scale, col_scale)


def text_rows(base, noise, col_scale):
    return (0.3 * base + noise) / math.sqrt(1.09) / math.sqrt(E) * col_scale


def draw_text(key, part):
    base, noise, row_scale, col_scale = shared_parts(key)
    text = text_rows(base, noise, col_scale)
    text = jnp.clip(text, -1.0, 1.0)
    return text.astype(jnp.bfloat16)


def draw_image(key, part):
    base, noise, row_scale, col_scale = shared_parts(key)
    image = base / math.sqrt(E) * row_scale
    image = jnp.clip(image, -6.0, 6.0)
    return image.astype(jnp.bfloat16)


def setup_inputs(seed: int = 0) -> dict:
    splits = jax.random.split(jax.random.key(seed), 4)
    image = draw_image(jax.random.fold_in(splits[3], 71), 0)
    text = draw_text(jax.random.fold_in(splits[3], 71), 0)
    logit_scale = jnp.clip(jnp.exp(jax.random.uniform(splits[2], (1,), jnp.float32, math.log(20.0), math.log(50.0))), 20.0, 50.0)
    return dict(image=image, text=text, logit_scale=logit_scale)


def reference(image, text, logit_scale):
    scale = logit_scale[0]
    total = image.shape[0]
    width = image.shape[1]
    block = math.gcd(total, 1024)
    count = total // block
    image_blocks = image.reshape(count, block, width)

    def forward(carry, piece):
        col_max, col_sum = carry
        s = scale * jnp.dot(piece, text.T, preferred_element_type=jnp.float32)
        row_part = jax.nn.logsumexp(s, axis=1)
        new_max = jnp.maximum(col_max, jnp.max(s, axis=0))
        col_sum = col_sum * jnp.exp(col_max - new_max) + jnp.sum(jnp.exp(s - new_max[None, :]), axis=0)
        return (new_max, col_sum), row_part

    init = (jnp.full((total,), -1e30, jnp.float32), jnp.zeros((total,), jnp.float32))
    (col_max, col_sum), row_parts = lax.scan(forward, init, image_blocks)
    row_lse = row_parts.reshape(total)
    col_lse = col_max + jnp.log(col_sum)
    diag = scale * jnp.sum(image.astype(jnp.float32) * text.astype(jnp.float32), axis=1)
    loss = ((jnp.sum(row_lse) + jnp.sum(col_lse) - 2.0 * jnp.sum(diag)) / (2.0 * total)).reshape(1)

    row_lse_blocks = row_lse.reshape(count, block)
    columns = lax.iota(jnp.int32, total)

    def backward(acc, xs):
        piece, lse_rows, index = xs
        s = scale * jnp.dot(piece, text.T, preferred_element_type=jnp.float32)
        rows = index * block + lax.iota(jnp.int32, block)
        eye = rows[:, None] == columns[None, :]
        g = 0.5 * (jnp.exp(s - lse_rows[:, None]) + jnp.exp(s - col_lse[None, :]))
        g = (g - jnp.where(eye, 1.0, 0.0)).astype(jnp.bfloat16)
        grad_rows = (scale * jnp.dot(g, text, preferred_element_type=jnp.float32)).astype(jnp.bfloat16)
        acc = acc + jnp.dot(g.T, piece, preferred_element_type=jnp.float32)
        return acc, grad_rows

    indices = lax.iota(jnp.int32, count)
    acc, grad_blocks = lax.scan(backward, jnp.zeros((total, width), jnp.float32), (image_blocks, row_lse_blocks, indices))
    grad_image = grad_blocks.reshape(total, width)
    grad_text = (scale * acc).astype(jnp.bfloat16)
    return loss, grad_image, grad_text
```

```python
import functools

import jax
import jax.numpy as jnp
from jax import lax
from jax.experimental import pallas as pl
from jax.experimental.pallas import tpu as pltpu
from jax.sharding import Mesh, PartitionSpec as P

AXES = ("x", "z", "yh", "yl", "c")
SIZES = (4, 4, 2, 2, 2)
PIECE = 96
CHIP = 2 * PIECE
KIND = 4 * CHIP
TILE = KIND // 2
WIDTH = 1024
EXTRA = 16
VMEM_LIMIT = 16 * 1024 * 1024

F32 = jnp.float32
BF16 = jnp.bfloat16
VMEM = pl.BlockSpec(memory_space=pltpu.VMEM)
SMEM = pl.BlockSpec(memory_space=pltpu.SMEM)


def pairs_of(move):
    def index(x, z, yh, yl, c):
        return (((x * 4 + z) * 2 + yh) * 2 + yl) * 2 + c

    return [
        (index(x, z, yh, yl, c), index(*move(x, z, yh, yl, c)))
        for x in range(4) for z in range(4) for yh in range(2) for yl in range(2) for c in range(2)
    ]


def on_ring(turn):
    return lambda x, z, yh, yl, c: (turn(x), z, yh, yl, c) if c == 0 else (x, turn(z), yh, yl, c)


AHEAD = [pairs_of(on_ring(lambda r, d=d: (r + d) % 4)) for d in range(4)]
PAIR_A = pairs_of(on_ring(lambda r: r ^ 1))
PAIR_B = pairs_of(on_ring(lambda r: r ^ 3))
flip_y = lambda x, z, yh, yl, c: (x, z, yh, 1 - yl, c) if c == 0 else (x, z, 1 - yh, yl, c)
FLIP_Y = pairs_of(flip_y)
CROSS_Y = pairs_of(lambda x, z, yh, yl, c: (*flip_y(x, z, yh, yl, c)[:4], 1 - c))
FLIP_YH = [(a, b) for a, b in FLIP_Y if a % 2 == 1]
FLIP_C = pairs_of(lambda x, z, yh, yl, c: (x, z, yh, yl, 1 - c))


def move(value, pairs):
    return lax.ppermute(value, AXES, pairs)


def call(body, out_shape, specs, scratch=(), flops=0, bytes_accessed=0, out_specs=None):
    return pl.pallas_call(
        body,
        out_shape=out_shape,
        in_specs=specs,
        out_specs=out_specs or jax.tree.map(lambda _: VMEM, out_shape),
        scratch_shapes=list(scratch),
        compiler_params=pltpu.CompilerParams(vmem_limit_bytes=VMEM_LIMIT),
        cost_estimate=pl.CostEstimate(flops=flops, bytes_accessed=bytes_accessed, transcendentals=0),
    )


def shape(*dims, dtype=F32):
    return jax.ShapeDtypeStruct(dims, dtype)


def lanes_of(s, combine):
    part = s[:, :128]
    for j in range(1, KIND // 128):
        part = combine(part, s[:, j * 128 : (j + 1) * 128])
    return part


def on_diagonal(j):
    row = lax.broadcasted_iota(jnp.int32, (TILE, 128), 0)
    return (row == lax.broadcasted_iota(jnp.int32, (TILE, 128), 1) + j * 128) & (row < CHIP)


def score_tiles(factor, rows, cols, s_ref, row_ref, col_max, col_sum):
    for r in range(2):
        part = slice(r * TILE, (r + 1) * TILE)
        s = factor * lax.dot_general(rows(part), cols(slice(None)), (((1,), (1,)), ((), ())), preferred_element_type=F32)
        s_ref[part, :] = s
        top = lanes_of(s, jnp.maximum)
        row_ref[0:1, part] = jnp.max(top.T, axis=0, keepdims=True)
        e = jnp.exp(s - jnp.max(top, axis=1, keepdims=True))
        row_ref[1:2, part] = jnp.sum(lanes_of(e, jnp.add).T, axis=0, keepdims=True)
        new_max = jnp.maximum(col_max, jnp.max(s, axis=0, keepdims=True))
        col_sum = col_sum * jnp.exp(col_max - new_max) + jnp.sum(jnp.exp(s - new_max), axis=0, keepdims=True)
        col_max = new_max
    return col_max, col_sum


def prepare(core, odd, image, text, text_c, first_ref, peer_ref):
    @pl.when(core[0] == 0)
    def _():
        first_ref[...] = image[...]
        peer_ref[:PIECE, :] = text[...]
        peer_ref[PIECE:, :] = text_c[...]

    @pl.when(core[0] == 1)
    def _():
        peer_ref[...] = image[...]
        first_ref[:PIECE, :] = text_c[...]
        first_ref[PIECE:, :] = text[...]


def scores_first(core, scale, *refs):
    a1, a2, b1 = refs[0:4], refs[4:8], refs[8:12]
    s_ref, x_ref, st_ref = refs[12:]
    me = core[0]
    for slot in range(4):
        at = slice(slot * CHIP, (slot + 1) * CHIP)
        x_ref[0, at, :] = b1[slot][...]

        @pl.when(me == 0)
        def _():
            x_ref[1, at, :] = a1[slot][...]

        @pl.when(me == 1)
        def _():
            x_ref[1, at, :] = a2[slot][...]

    st_ref[...] = jnp.ones((8, KIND), F32)
    col_max, col_sum = score_tiles(
        scale[0],
        lambda part: x_ref[1 - me, part, :],
        lambda part: x_ref[me, part, :],
        s_ref,
        st_ref,
        jnp.full((1, KIND), -1e30, F32),
        jnp.zeros((1, KIND), F32),
    )
    st_ref[4:5, :] = col_max
    st_ref[5:6, :] = col_sum
    total = jnp.zeros((1, 1), F32)
    for j in range(2):
        here = jnp.where(on_diagonal(j), s_ref[:TILE, j * 128 : (j + 1) * 128], 0.0)
        total += jnp.sum(jnp.sum(here, axis=0, keepdims=True), axis=1, keepdims=True)
    st_ref[6:7, :] = jnp.broadcast_to(total, (1, KIND))


def scores_second(core, scale, x_ref, st1, *refs):
    a2, text0, b2 = refs[0:4], refs[4], refs[5:8]
    s_ref, y_ref, st_ref, line = refs[8:]
    me = core[0]

    @pl.when(me == 0)
    def _():
        y_ref[0, :CHIP, :] = text0[...]
        for slot in range(4):
            y_ref[1, slot * CHIP : (slot + 1) * CHIP, :] = a2[slot][...]

    @pl.when(me == 1)
    def _():
        y_ref[0, :CHIP, :] = a2[0][...]

    for slot in range(1, 4):
        y_ref[0, slot * CHIP : (slot + 1) * CHIP, :] = b2[slot - 1][...]

    col_max, col_sum = score_tiles(
        scale[0],
        lambda part: y_ref[1 - me, part, :],
        lambda part: x_ref[me, part, :],
        s_ref,
        line,
        st1[4:5, :],
        st1[5:6, :],
    )
    st_ref[...] = jnp.concatenate(
        [st1[0:1, :], line[0:1, :], st1[1:2, :], line[1:2, :], col_max, col_sum, st1[6:8, :]], axis=0
    )


def join(a, b):
    top = jnp.maximum(a[0:2], b[0:2])
    total = a[2:4] * jnp.exp(a[0:2] - top) + b[2:4] * jnp.exp(b[0:2] - top)
    return jnp.concatenate([top, total, a[4:5] + b[4:5], jnp.ones((3, KIND), F32)], axis=0)


def join_cores(core, mine_ref, peer_ref, *refs):
    o_ref = refs[-1]
    a, b = mine_ref[...], peer_ref[...]
    rows = join(a[0:5], b[0:5])
    rows = jnp.concatenate([rows[0:4], a[6:7], rows[5:8]], axis=0)
    cols = jnp.concatenate([b[4:5], a[4:5], b[5:6], a[5:6], jnp.zeros((1, KIND), F32), rows[5:8]], axis=0)
    o_ref[...] = jnp.where(core[0] == 0, rows, cols)


def join_pair(a_ref, b_ref, *refs):
    o_ref = refs[-1]
    b = b_ref[...]
    o_ref[...] = join(a_ref[...], jnp.concatenate([b[1:2], b[0:1], b[3:4], b[2:3], b[4:8]], axis=0))


def join_ring(last, odd, a_ref, b_ref, *refs):
    o_ref = refs[-1]
    b = b_ref[...]
    one = jnp.concatenate([b[:, KIND - CHIP :], b[:, : KIND - CHIP]], axis=1)
    three = jnp.concatenate([b[:, CHIP:], b[:, :CHIP]], axis=1)
    out = join(a_ref[...], jnp.where((odd[0] == 1) == last, one, three))
    if last:
        out = jnp.concatenate([out[0:2] + jnp.log(out[2:4]), out[2:8]], axis=0)
    o_ref[...] = out


def grad_weights(kind, core, s_ref, mine_ref, peer_ref, g_ref):
    image = core[0] == 0
    rows = jnp.where(image, mine_ref[kind : kind + 1, :], peer_ref[kind : kind + 1, :])
    cols = jnp.where(image, peer_ref[0:1, :], mine_ref[1:2, :])
    for r in range(2):
        lse = jnp.broadcast_to(rows[:, r * TILE : (r + 1) * TILE], (128, TILE)).T
        for j in range(KIND // 128):
            at = slice(j * 128, (j + 1) * 128)
            s = s_ref[r * TILE : (r + 1) * TILE, at]
            g = 0.5 * (jnp.exp(s - lse) + jnp.exp(s - cols[:, at]))
            if kind == 0 and r == 0 and j < 2:
                g = g - jnp.where(on_diagonal(j) & image, 1.0, 0.0)
            g_ref[r * TILE : (r + 1) * TILE, at] = g.astype(BF16)


def spread(value):
    high = value.astype(BF16).astype(F32)
    middle = (value - high).astype(BF16).astype(F32)
    low = value - high - middle
    lane = lax.broadcasted_iota(jnp.int32, (EXTRA, WIDTH), 1)
    out = jnp.where(lane < 128, high, jnp.where(lane < 256, middle, low))
    return out.astype(BF16)


def gathered(rows):
    rows = rows[0:1, :].astype(F32)
    return rows[:, 0:1] + rows[:, 128:129] + rows[:, 256:257]


def product(core, half, left, left_t, first, second, outs):
    at = slice(half * TILE, (half + 1) * TILE)

    def write(out):
        for k in range(2):
            value = out[k * CHIP : (k + 1) * CHIP, :]
            outs[k][0:CHIP, :] = value if (half, k) == (0, 0) else value.astype(BF16)

    @pl.when(core[0] == 0)
    def _():
        out = jnp.dot(left[0][at, :], first[0], preferred_element_type=F32)
        write(out + jnp.dot(left[1][at, :], second[0], preferred_element_type=F32))

    @pl.when(core[0] == 1)
    def _():
        over = (((0,), (0,)), ((), ()))
        out = lax.dot_general(left_t[0][:, at], first[0], over, preferred_element_type=F32)
        write(out + lax.dot_general(left_t[1][:, at], second[0], over, preferred_element_type=F32))


def grads_other(half, core, g1, g2, r2, x_ref, y_ref, mine_ref, peer_ref, *outs):
    product(core, half, (g2, r2), (g1, g2), x_ref, y_ref, outs)
    peer = peer_ref[...]
    term = jnp.sum(jnp.sum(peer[0:2], axis=0, keepdims=True), axis=1, keepdims=True)
    term = term - jnp.where(core[0] == 0, 0.0, 2.0 * peer[4:5, 0:1])
    if half == 0:
        outs[2][...] = jnp.broadcast_to(term, (8, 128))
    for out in outs[1 - half : 2]:
        out[CHIP:, :] = spread(term)


def grads_own(half, core, g1, r1, r2, x_ref, y_ref, *outs):
    product(core, half, (g1, r1), (r1, r2), x_ref, y_ref, outs)


def sum_other(core, acc, r1, r2, r3, term, *refs):
    same_ref, cross_ref, total_ref = refs[-3:]
    out = acc[...]
    total = term[0:1, 0:1]
    for r in (r1, r2, r3):
        out = out + r[0:CHIP, :].astype(F32)
        total = total + gathered(r[CHIP:, :])
    low, high = out[:PIECE].astype(BF16), out[PIECE:].astype(BF16)
    image = core[0] == 0
    same_ref[...] = jnp.where(image, low, high)
    cross_ref[...] = jnp.where(image, high, low)
    total_ref[...] = jnp.broadcast_to(total, (8, 128))


def sum_own(core, acc, r1, r2, r3, total, pair_total, keep_ref, give_a_ref, give_b_ref, total_ref):
    out = acc[...]
    for r in (r1, r2, r3):
        out = out + r[...].astype(F32)
    low, high = out[:PIECE], out[PIECE:]
    image = core[0] == 0
    keep_ref[...] = jnp.where(image, low, high)
    give = jnp.where(image, high, low).astype(BF16)
    whole = total[...] + pair_total[...]
    give_a_ref[0 : PIECE // 2, :] = give[: PIECE // 2]
    give_a_ref[PIECE // 2 :, :] = spread(whole[0:1, 0:1])
    give_b_ref[...] = give[PIECE // 2 :]
    total_ref[...] = whole


def finish(core, scale, keep, got_a, got_b, same, cross, total, image_ref, text_ref, loss_ref):
    mine = (scale[0] * (keep[...] + same[...].astype(F32))).astype(BF16)
    got = jnp.concatenate([got_a[: PIECE // 2, :], got_b[...]], axis=0)
    other = (scale[0] * (got.astype(F32) + cross[...].astype(F32))).astype(BF16)
    image = core[0] == 0
    image_ref[...] = jnp.where(image, mine, other)
    text_ref[...] = jnp.where(image, other, mine)
    loss = total[0:1, 0:1] + gathered(got_a[PIECE // 2 :, :])
    loss_ref[0] = loss[0, 0] / (16.0 * 2 * KIND)


def on_device(image, text, logit_scale):
    c = lax.axis_index("c")
    yl = lax.axis_index("yl")
    is_image = c == 0
    ring = jnp.where(is_image, lax.axis_index("x"), lax.axis_index("z"))
    core = c.reshape(1)
    odd = (ring & 1).reshape(1)
    mat = functools.partial(shape, dtype=BF16)

    chip = mat(CHIP, WIDTH)
    image_own = lax.dynamic_slice_in_dim(image, yl * CHIP, CHIP, 0)
    image_other = lax.dynamic_slice_in_dim(image, (1 - yl) * CHIP, CHIP, 0)
    image_own, image_other = lax.optimization_barrier((image_own, image_other))
    first, peer_first = call(prepare, (chip, chip), [SMEM] * 2 + [VMEM] * 3)(core, odd, image_own, text, move(text, FLIP_C))
    text_y = move(first, FLIP_YH)
    ring1 = [move(first, AHEAD[4 - slot]) for slot in (1, 2, 3)]
    second = jnp.where(is_image, image_other, text_y)
    ring2 = [move(second, AHEAD[4 - slot]) for slot in (1, 2, 3)]
    peer1 = [move(v, FLIP_C) for v in ring1]
    text_yc = move(text_y, FLIP_C)
    peer2 = [move(v, FLIP_C) for v in ring2]

    half = 2 * KIND * KIND * WIDTH
    s1, x, st1 = call(
        scores_first,
        (shape(KIND, KIND), mat(2, KIND, WIDTH), shape(8, KIND)),
        [SMEM] * 2 + [VMEM] * 12,
        flops=half,
        bytes_accessed=KIND * KIND * 4,
    )(core, logit_scale, first, *ring1, second, *ring2, peer_first, *peer1)
    s2, y, st = call(
        scores_second,
        (shape(KIND, KIND), mat(2, KIND, WIDTH), shape(8, KIND)),
        [SMEM] * 2 + [VMEM] * 10,
        scratch=[pltpu.VMEM((8, KIND), F32)],
        flops=half,
        bytes_accessed=KIND * KIND * 4,
    )(core, logit_scale, x, st1, image_other, *ring2, text_yc, *peer2)

    stats = shape(8, KIND)
    held = (s1, s2, x, y)
    side = call(join_cores, stats, [SMEM] + [VMEM] * 6)(core, st, move(st, FLIP_C), *held)
    side = call(join_pair, stats, [VMEM] * 6)(side, move(side, FLIP_Y), *held)
    side = call(functools.partial(join_ring, False), stats, [SMEM] + [VMEM] * 6)(odd, side, move(side, PAIR_A), *held)
    side = call(functools.partial(join_ring, True), stats, [SMEM] + [VMEM] * 6)(odd, side, move(side, PAIR_B), *held)
    peer = move(side, FLIP_C)

    weights = lambda kind, s: call(functools.partial(grad_weights, kind), mat(KIND, KIND), [SMEM] + [VMEM] * 3)(
        core, s, side, peer
    )
    g2 = weights(1, s2)
    r2 = move(g2, FLIP_C)
    g1 = weights(0, s1)
    r1 = move(g1, FLIP_C)
    long, own, small = mat(CHIP + EXTRA, WIDTH), shape(CHIP, WIDTH), shape(8, 128)

    def grads(body, out_shape, *operands):
        return call(body, out_shape, [SMEM] + [VMEM] * len(operands), flops=half)(core, *operands)

    send_2, send_3 = grads(functools.partial(grads_other, 1), (long, long), g1, g2, r2, x, y, side, peer)
    acc2, send_1, term = grads(functools.partial(grads_other, 0), (own, long, small), g1, g2, r2, x, y, side, peer)
    got2 = [move(v, AHEAD[k + 1]) for k, v in enumerate((send_1, send_2, send_3))]
    send_2, send_3 = grads(functools.partial(grads_own, 1), (chip, chip), g1, r1, r2, x, y)
    acc1, send_1 = grads(functools.partial(grads_own, 0), (own, chip), g1, r1, r2, x, y)
    got1 = [move(v, AHEAD[k + 1]) for k, v in enumerate((send_1, send_2, send_3))]
    piece, part = mat(PIECE, WIDTH), mat(PIECE // 2, WIDTH)
    same, cross, total = call(sum_other, (piece, piece, small), [SMEM] + [VMEM] * 7)(core, acc2, *got2, term, send_2, acc1)
    pair_total = move(total, FLIP_Y)
    same, cross = move(same, FLIP_Y), move(cross, CROSS_Y)
    keep, give_a, give_b, total = call(
        sum_own, (shape(PIECE, WIDTH), mat(PIECE // 2 + EXTRA, WIDTH), part, small), [SMEM] + [VMEM] * 6
    )(core, acc1, *got1, total, pair_total)
    grad_image, grad_text, loss = call(
        finish, (piece, piece, shape(1)), [SMEM] * 2 + [VMEM] * 6, out_specs=(VMEM, VMEM, SMEM)
    )(core, logit_scale, keep, move(give_a, FLIP_C), move(give_b, FLIP_C), same, cross, total)
    return loss, grad_image, grad_text


def solution(mesh):
    fine = Mesh(mesh.devices.reshape(SIZES), AXES)
    every = P(AXES, None)
    return jax.shard_map(
        on_device,
        mesh=fine,
        in_specs=(P(("x", "z", "yh"), None), every, P()),
        out_specs=(P(), every, every),
        check_vma=False,
    )
```

```python
import functools

import jax
import jax.numpy as jnp
from jax import lax
from jax.experimental import pallas as pl
from jax.experimental.pallas import tpu as pltpu
from jax.sharding import Mesh, PartitionSpec as P

AXES = ("x", "z", "yh", "yl", "c")
SIZES = (4, 4, 2, 2, 2)
PIECE = 96
CHIP = 2 * PIECE
KIND = 4 * CHIP
TILE = KIND // 2
WIDTH = 1024
EXTRA = 16
VMEM_LIMIT = 16 * 1024 * 1024

F32 = jnp.float32
BF16 = jnp.bfloat16
VMEM = pl.BlockSpec(memory_space=pltpu.VMEM)
SMEM = pl.BlockSpec(memory_space=pltpu.SMEM)


def pairs_of(move):
    def index(x, z, yh, yl, c):
        return (((x * 4 + z) * 2 + yh) * 2 + yl) * 2 + c

    return [
        (index(x, z, yh, yl, c), index(*move(x, z, yh, yl, c)))
        for x in range(4) for z in range(4) for yh in range(2) for yl in range(2) for c in range(2)
    ]


def on_ring(turn):
    return lambda x, z, yh, yl, c: (turn(x), z, yh, yl, c) if c == 0 else (x, turn(z), yh, yl, c)


AHEAD = [pairs_of(on_ring(lambda r, d=d: (r + d) % 4)) for d in range(4)]
PAIR_A = pairs_of(on_ring(lambda r: r ^ 1))
PAIR_B = pairs_of(on_ring(lambda r: r ^ 3))
flip_y = lambda x, z, yh, yl, c: (x, z, yh, 1 - yl, c) if c == 0 else (x, z, 1 - yh, 1 - yl, c)
FLIP_Y = pairs_of(flip_y)
CROSS_Y = pairs_of(lambda x, z, yh, yl, c: (*flip_y(x, z, yh, yl, c)[:4], 1 - c))
FLIP_YH = [(a, b) for a, b in FLIP_Y if a % 2 == 1]
FLIP_C = pairs_of(lambda x, z, yh, yl, c: (x, z, yh, yl, 1 - c))


def move(value, pairs):
    return lax.ppermute(value, AXES, pairs)


def call(body, out_shape, specs, scratch=(), flops=0, bytes_accessed=0, out_specs=None):
    return pl.pallas_call(
        body,
        out_shape=out_shape,
        in_specs=specs,
        out_specs=out_specs or jax.tree.map(lambda _: VMEM, out_shape),
        scratch_shapes=list(scratch),
        compiler_params=pltpu.CompilerParams(vmem_limit_bytes=VMEM_LIMIT),
        cost_estimate=pl.CostEstimate(flops=flops, bytes_accessed=bytes_accessed, transcendentals=0),
    )


def shape(*dims, dtype=F32):
    return jax.ShapeDtypeStruct(dims, dtype)


def lanes_of(s, combine):
    part = s[:, :128]
    for j in range(1, KIND // 128):
        part = combine(part, s[:, j * 128 : (j + 1) * 128])
    return part


def on_diagonal(j):
    row = lax.broadcasted_iota(jnp.int32, (TILE, 128), 0)
    return (row == lax.broadcasted_iota(jnp.int32, (TILE, 128), 1) + j * 128) & (row < CHIP)


def score_tiles(factor, rows, cols, s_ref, row_ref, col_max, col_sum):
    for r in range(2):
        part = slice(r * TILE, (r + 1) * TILE)
        s = factor * lax.dot_general(rows(part), cols(slice(None)), (((1,), (1,)), ((), ())), preferred_element_type=F32)
        s_ref[part, :] = s
        top = lanes_of(s, jnp.maximum)
        row_ref[0:1, part] = jnp.max(top.T, axis=0, keepdims=True)
        e = jnp.exp(s - jnp.max(top, axis=1, keepdims=True))
        row_ref[1:2, part] = jnp.sum(lanes_of(e, jnp.add).T, axis=0, keepdims=True)
        new_max = jnp.maximum(col_max, jnp.max(s, axis=0, keepdims=True))
        col_sum = col_sum * jnp.exp(col_max - new_max) + jnp.sum(jnp.exp(s - new_max), axis=0, keepdims=True)
        col_max = new_max
    return col_max, col_sum


def prepare(core, odd, image, text, text_c, first_ref, peer_ref):
    @pl.when(core[0] == 0)
    def _():
        first_ref[...] = image[...]
        peer_ref[:PIECE, :] = text[...]
        peer_ref[PIECE:, :] = text_c[...]

    @pl.when(core[0] == 1)
    def _():
        peer_ref[...] = image[...]
        first_ref[:PIECE, :] = text_c[...]
        first_ref[PIECE:, :] = text[...]


def scores_first(core, scale, *refs):
    a1, a2, b1 = refs[0:4], refs[4:8], refs[8:12]
    s_ref, x_ref, st_ref = refs[12:]
    me = core[0]
    for slot in range(4):
        at = slice(slot * CHIP, (slot + 1) * CHIP)
        x_ref[0, at, :] = b1[slot][...]

        @pl.when(me == 0)
        def _():
            x_ref[1, at, :] = a1[slot][...]

        @pl.when(me == 1)
        def _():
            x_ref[1, at, :] = a2[slot][...]

    st_ref[...] = jnp.ones((8, KIND), F32)
    col_max, col_sum = score_tiles(
        scale[0],
        lambda part: x_ref[1 - me, part, :],
        lambda part: x_ref[me, part, :],
        s_ref,
        st_ref,
        jnp.full((1, KIND), -1e30, F32),
        jnp.zeros((1, KIND), F32),
    )
    st_ref[4:5, :] = col_max
    st_ref[5:6, :] = col_sum
    total = jnp.zeros((1, 1), F32)
    for j in range(2):
        here = jnp.where(on_diagonal(j), s_ref[:TILE, j * 128 : (j + 1) * 128], 0.0)
        total += jnp.sum(jnp.sum(here, axis=0, keepdims=True), axis=1, keepdims=True)
    st_ref[6:7, :] = jnp.broadcast_to(total, (1, KIND))


def scores_second(core, scale, x_ref, st1, *refs):
    a2, text0, b2 = refs[0:4], refs[4], refs[5:8]
    s_ref, y_ref, st_ref, line = refs[8:]
    me = core[0]

    @pl.when(me == 0)
    def _():
        y_ref[0, :CHIP, :] = text0[...]
        for slot in range(4):
            y_ref[1, slot * CHIP : (slot + 1) * CHIP, :] = a2[slot][...]

    @pl.when(me == 1)
    def _():
        y_ref[0, :CHIP, :] = a2[0][...]

    for slot in range(1, 4):
        y_ref[0, slot * CHIP : (slot + 1) * CHIP, :] = b2[slot - 1][...]

    col_max, col_sum = score_tiles(
        scale[0],
        lambda part: y_ref[1 - me, part, :],
        lambda part: x_ref[me, part, :],
        s_ref,
        line,
        st1[4:5, :],
        st1[5:6, :],
    )
    st_ref[...] = jnp.concatenate(
        [st1[0:1, :], line[0:1, :], st1[1:2, :], line[1:2, :], col_max, col_sum, st1[6:8, :]], axis=0
    )


def join(a, b):
    top = jnp.maximum(a[0:2], b[0:2])
    total = a[2:4] * jnp.exp(a[0:2] - top) + b[2:4] * jnp.exp(b[0:2] - top)
    return jnp.concatenate([top, total, a[4:5] + b[4:5], jnp.ones((3, KIND), F32)], axis=0)


def join_cores(core, mine_ref, peer_ref, *refs):
    o_ref = refs[-1]
    a, b = mine_ref[...], peer_ref[...]
    rows = join(a[0:5], b[0:5])
    rows = jnp.concatenate([rows[0:4], a[6:7], rows[5:8]], axis=0)
    cols = jnp.concatenate([b[4:5], a[4:5], b[5:6], a[5:6], jnp.zeros((1, KIND), F32), rows[5:8]], axis=0)
    o_ref[...] = jnp.where(core[0] == 0, rows, cols)


def join_pair(a_ref, b_ref, *refs):
    o_ref = refs[-1]
    b = b_ref[...]
    o_ref[...] = join(a_ref[...], jnp.concatenate([b[1:2], b[0:1], b[3:4], b[2:3], b[4:8]], axis=0))


def join_ring(a_ref, b1_ref, b2_ref, b3_ref, *refs):
    out = a_ref[...]
    for k, b_ref in enumerate((b1_ref, b2_ref, b3_ref)):
        b, cut = b_ref[...], KIND - (k + 1) * CHIP
        out = join(out, jnp.concatenate([b[:, cut:], b[:, :cut]], axis=1))
    refs[-1][...] = jnp.concatenate([out[0:2] + jnp.log(out[2:4]), out[2:8]], axis=0)


def grad_weights(kind, core, s_ref, mine_ref, peer_ref, g_ref):
    image = core[0] == 0
    rows = jnp.where(image, mine_ref[kind : kind + 1, :], peer_ref[kind : kind + 1, :])
    cols = jnp.where(image, peer_ref[0:1, :], mine_ref[1:2, :])
    for r in range(2):
        lse = jnp.broadcast_to(rows[:, r * TILE : (r + 1) * TILE], (128, TILE)).T
        for j in range(KIND // 128):
            at = slice(j * 128, (j + 1) * 128)
            s = s_ref[r * TILE : (r + 1) * TILE, at]
            g = 0.5 * (jnp.exp(s - lse) + jnp.exp(s - cols[:, at]))
            if kind == 0 and r == 0 and j < 2:
                g = g - jnp.where(on_diagonal(j) & image, 1.0, 0.0)
            g_ref[r * TILE : (r + 1) * TILE, at] = g.astype(BF16)


def spread(value):
    high = value.astype(BF16).astype(F32)
    middle = (value - high).astype(BF16).astype(F32)
    low = value - high - middle
    lane = lax.broadcasted_iota(jnp.int32, (EXTRA, WIDTH), 1)
    out = jnp.where(lane < 128, high, jnp.where(lane < 256, middle, low))
    return out.astype(BF16)


def gathered(rows):
    rows = rows[0:1, :].astype(F32)
    return rows[:, 0:1] + rows[:, 128:129] + rows[:, 256:257]


def product(core, half, left, left_t, first, second, outs):
    at = slice(half * TILE, (half + 1) * TILE)

    def write(out):
        for k in range(2):
            value = out[k * CHIP : (k + 1) * CHIP, :]
            outs[k][0:CHIP, :] = value if (half, k) == (0, 0) else value.astype(BF16)

    @pl.when(core[0] == 0)
    def _():
        out = jnp.dot(left[0][at, :], first[0], preferred_element_type=F32)
        write(out + jnp.dot(left[1][at, :], second[0], preferred_element_type=F32))

    @pl.when(core[0] == 1)
    def _():
        over = (((0,), (0,)), ((), ()))
        out = lax.dot_general(left_t[0][:, at], first[0], over, preferred_element_type=F32)
        write(out + lax.dot_general(left_t[1][:, at], second[0], over, preferred_element_type=F32))


def grads_other(half, core, g1, g2, r2, x_ref, y_ref, mine_ref, peer_ref, *outs):
    product(core, half, (g2, r2), (g1, g2), x_ref, y_ref, outs)
    peer = peer_ref[...]
    term = jnp.sum(jnp.sum(peer[0:2], axis=0, keepdims=True), axis=1, keepdims=True)
    term = term - jnp.where(core[0] == 0, 0.0, 2.0 * peer[4:5, 0:1])
    if half == 0:
        outs[2][...] = jnp.broadcast_to(term, (8, 128))
    for out in outs[1 - half : 2]:
        out[CHIP:, :] = spread(term)


def grads_own(half, core, g1, r1, r2, x_ref, y_ref, *outs):
    product(core, half, (g1, r1), (r1, r2), x_ref, y_ref, outs)


def sum_other(core, acc, r1, r2, r3, term, *refs):
    same_ref, cross_ref, total_ref = refs[-3:]
    out = acc[...]
    total = term[0:1, 0:1]
    for r in (r1, r2, r3):
        out = out + r[0:CHIP, :].astype(F32)
        total = total + gathered(r[CHIP:, :])
    low, high = out[:PIECE].astype(BF16), out[PIECE:].astype(BF16)
    image = core[0] == 0
    same_ref[...] = jnp.where(image, low, high)
    cross_ref[...] = jnp.where(image, high, low)
    total_ref[...] = jnp.broadcast_to(total, (8, 128))


def sum_own(core, acc, r1, r2, r3, total, pair_total, keep_ref, give_a_ref, give_b_ref, total_ref):
    out = acc[...]
    for r in (r1, r2, r3):
        out = out + r[...].astype(F32)
    low, high = out[:PIECE], out[PIECE:]
    image = core[0] == 0
    keep_ref[...] = jnp.where(image, low, high)
    give = jnp.where(image, high, low).astype(BF16)
    whole = total[...] + pair_total[...]
    give_a_ref[0 : PIECE // 2, :] = give[: PIECE // 2]
    give_a_ref[PIECE // 2 :, :] = spread(whole[0:1, 0:1])
    give_b_ref[...] = give[PIECE // 2 :]
    total_ref[...] = whole


def finish(core, scale, keep, got_a, got_b, same, cross, total, image_ref, text_ref, loss_ref):
    mine = (scale[0] * (keep[...] + same[...].astype(F32))).astype(BF16)
    got = jnp.concatenate([got_a[: PIECE // 2, :], got_b[...]], axis=0)
    other = (scale[0] * (got.astype(F32) + cross[...].astype(F32))).astype(BF16)
    image = core[0] == 0
    image_ref[...] = jnp.where(image, mine, other)
    text_ref[...] = jnp.where(image, other, mine)
    loss = total[0:1, 0:1] + gathered(got_a[PIECE // 2 :, :])
    loss_ref[0] = loss[0, 0] / (16.0 * 2 * KIND)


def on_device(image, text, logit_scale):
    c = lax.axis_index("c")
    yl = lax.axis_index("yl")
    is_image = c == 0
    ring = jnp.where(is_image, lax.axis_index("x"), lax.axis_index("z"))
    core = c.reshape(1)
    odd = (ring & 1).reshape(1)
    mat = functools.partial(shape, dtype=BF16)

    chip = mat(CHIP, WIDTH)
    image_own = lax.dynamic_slice_in_dim(image, yl * CHIP, CHIP, 0)
    image_other = lax.dynamic_slice_in_dim(image, (1 - yl) * CHIP, CHIP, 0)
    image_own, image_other = lax.optimization_barrier((image_own, image_other))
    first, peer_first = call(prepare, (chip, chip), [SMEM] * 2 + [VMEM] * 3)(core, odd, image_own, text, move(text, FLIP_C))
    text_y = move(first, FLIP_YH)
    ring1 = [move(first, AHEAD[4 - slot]) for slot in (1, 2, 3)]
    second = jnp.where(is_image, image_other, text_y)
    ring2 = [move(second, AHEAD[3]), move(ring1[1], FLIP_Y), move(second, AHEAD[1])]
    ring1[0], ring1[1], ring1[2], ring2[1] = lax.optimization_barrier((*ring1, ring2[1]))
    peer1 = [move(v, FLIP_C) for v in ring1]
    text_yc = move(text_y, FLIP_C)
    peer2 = [move(v, FLIP_C) for v in ring2]

    half = 2 * KIND * KIND * WIDTH
    s1, x, st1 = call(
        scores_first,
        (shape(KIND, KIND), mat(2, KIND, WIDTH), shape(8, KIND)),
        [SMEM] * 2 + [VMEM] * 12,
        flops=half,
        bytes_accessed=KIND * KIND * 4,
    )(core, logit_scale, first, *ring1, second, *ring2, peer_first, *peer1)
    s2, y, st = call(
        scores_second,
        (shape(KIND, KIND), mat(2, KIND, WIDTH), shape(8, KIND)),
        [SMEM] * 2 + [VMEM] * 10,
        scratch=[pltpu.VMEM((8, KIND), F32)],
        flops=half,
        bytes_accessed=KIND * KIND * 4,
    )(core, logit_scale, x, st1, image_other, *ring2, text_yc, *peer2)

    stats = shape(8, KIND)
    held = (s1, s2, x, y)
    side = call(join_cores, stats, [SMEM] + [VMEM] * 6)(core, st, move(st, FLIP_C), *held)
    side = call(join_pair, stats, [VMEM] * 6)(side, move(side, FLIP_Y), *held)
    others = [move(side, AHEAD[4 - k]) for k in (1, 2, 3)]
    side = call(join_ring, stats, [VMEM] * 8)(side, *others, *held)
    peer = move(side, FLIP_C)

    weights = lambda kind, s: call(functools.partial(grad_weights, kind), mat(KIND, KIND), [SMEM] + [VMEM] * 3)(
        core, s, side, peer
    )
    g2 = weights(1, s2)
    r2 = move(g2, FLIP_C)
    g1 = weights(0, s1)
    r1 = move(g1, FLIP_C)
    long, own, small = mat(CHIP + EXTRA, WIDTH), shape(CHIP, WIDTH), shape(8, 128)

    def grads(body, out_shape, *operands):
        return call(body, out_shape, [SMEM] + [VMEM] * len(operands), flops=half)(core, *operands)

    send_2, send_3 = grads(functools.partial(grads_other, 1), (long, long), g1, g2, r2, x, y, side, peer)
    acc2, send_1, term = grads(functools.partial(grads_other, 0), (own, long, small), g1, g2, r2, x, y, side, peer)
    got2 = [move(v, AHEAD[k + 1]) for k, v in enumerate((send_1, send_2, send_3))]
    send_2, send_3 = grads(functools.partial(grads_own, 1), (chip, chip), g1, r1, r2, x, y)
    acc1, send_1 = grads(functools.partial(grads_own, 0), (own, chip), g1, r1, r2, x, y)
    got1 = [move(v, AHEAD[k + 1]) for k, v in enumerate((send_1, send_2, send_3))]
    piece, part = mat(PIECE, WIDTH), mat(PIECE // 2, WIDTH)
    same, cross, total = call(sum_other, (piece, piece, small), [SMEM] + [VMEM] * 7)(core, acc2, *got2, term, send_2, acc1)
    pair_total = move(total, FLIP_Y)
    same, cross = move(same, FLIP_Y), move(cross, CROSS_Y)
    keep, give_a, give_b, total = call(
        sum_own, (shape(PIECE, WIDTH), mat(PIECE // 2 + EXTRA, WIDTH), part, small), [SMEM] + [VMEM] * 6
    )(core, acc1, *got1, total, pair_total)
    grad_image, grad_text, loss = call(
        finish, (piece, piece, shape(1)), [SMEM] * 2 + [VMEM] * 6, out_specs=(VMEM, VMEM, SMEM)
    )(core, logit_scale, keep, move(give_a, FLIP_C), move(give_b, FLIP_C), same, cross, total)
    return loss, grad_image, grad_text


def solution(mesh):
    fine = Mesh(mesh.devices.reshape(SIZES), AXES)
    every = P(AXES, None)
    return jax.shard_map(
        on_device,
        mesh=fine,
        in_specs=(P(("x", "z", "yh"), None), every, P()),
        out_specs=(P(), every, every),
        check_vma=False,
    )
```

```python
import functools

import jax
import jax.numpy as jnp
from jax import lax
from jax.experimental import pallas as pl
from jax.experimental.pallas import tpu as pltpu
from jax.sharding import Mesh, PartitionSpec as P

AXES = ("x", "z", "yh", "yl", "c")
SIZES = (4, 4, 2, 2, 2)
PIECE = 96
CHIP = 2 * PIECE
KIND = 4 * CHIP
TILE = KIND // 2
WIDTH = 1024
EXTRA = 16
VMEM_LIMIT = 16 * 1024 * 1024

F32 = jnp.float32
BF16 = jnp.bfloat16
VMEM = pl.BlockSpec(memory_space=pltpu.VMEM)
SMEM = pl.BlockSpec(memory_space=pltpu.SMEM)


def pairs_of(move):
    def index(x, z, yh, yl, c):
        return (((x * 4 + z) * 2 + yh) * 2 + yl) * 2 + c

    return [
        (index(x, z, yh, yl, c), index(*move(x, z, yh, yl, c)))
        for x in range(4) for z in range(4) for yh in range(2) for yl in range(2) for c in range(2)
    ]


def on_ring(turn):
    return lambda x, z, yh, yl, c: (turn(x), z, yh, yl, c) if c == 0 else (x, turn(z), yh, yl, c)


AHEAD = [pairs_of(on_ring(lambda r, d=d: (r + d) % 4)) for d in range(4)]
ahead_one = on_ring(lambda r: (r + 1) % 4)
AHEAD_CROSS = pairs_of(lambda x, z, yh, yl, c: (*ahead_one(x, z, yh, yl, c)[:4], 1 - c))
flip_y = lambda x, z, yh, yl, c: (x, z, yh, 1 - yl, c) if c == 0 else (x, z, 1 - yh, 1 - yl, c)
FLIP_Y = pairs_of(flip_y)
CROSS_Y = pairs_of(lambda x, z, yh, yl, c: (*flip_y(x, z, yh, yl, c)[:4], 1 - c))
FLIP_YH = [(a, b) for a, b in FLIP_Y if a % 2 == 1]
FLIP_C = pairs_of(lambda x, z, yh, yl, c: (x, z, yh, yl, 1 - c))


def move(value, pairs):
    return lax.ppermute(value, AXES, pairs)


def call(body, out_shape, specs, scratch=(), flops=0, bytes_accessed=0, out_specs=None):
    return pl.pallas_call(
        body,
        out_shape=out_shape,
        in_specs=specs,
        out_specs=out_specs or jax.tree.map(lambda _: VMEM, out_shape),
        scratch_shapes=list(scratch),
        compiler_params=pltpu.CompilerParams(vmem_limit_bytes=VMEM_LIMIT),
        cost_estimate=pl.CostEstimate(flops=flops, bytes_accessed=bytes_accessed, transcendentals=0),
    )


def shape(*dims, dtype=F32):
    return jax.ShapeDtypeStruct(dims, dtype)


def lanes_of(s, combine):
    part = s[:, :128]
    for j in range(1, KIND // 128):
        part = combine(part, s[:, j * 128 : (j + 1) * 128])
    return part


def on_diagonal(j):
    row = lax.broadcasted_iota(jnp.int32, (TILE, 128), 0)
    return (row == lax.broadcasted_iota(jnp.int32, (TILE, 128), 1) + j * 128) & (row < CHIP)


def score_tiles(factor, rows, cols, s_ref, row_ref, col_max, col_sum):
    for r in range(3):
        part = slice(r * 256, (r + 1) * 256)
        s = factor * lax.dot_general(rows(part), cols(slice(None)), (((1,), (1,)), ((), ())), preferred_element_type=F32)
        s_ref[part, :] = s
        top = lanes_of(s, jnp.maximum)
        row_ref[0:1, part] = jnp.max(top.T, axis=0, keepdims=True)
        e = jnp.exp(s - jnp.max(top, axis=1, keepdims=True))
        row_ref[1:2, part] = jnp.sum(lanes_of(e, jnp.add).T, axis=0, keepdims=True)
        new_max = jnp.maximum(col_max, jnp.max(s, axis=0, keepdims=True))
        col_sum = col_sum * jnp.exp(col_max - new_max) + jnp.sum(jnp.exp(s - new_max), axis=0, keepdims=True)
        col_max = new_max
    return col_max, col_sum


def prepare(core, odd, image, text, text_c, first_ref, peer_ref):
    @pl.when(core[0] == 0)
    def _():
        first_ref[...] = image[...]
        peer_ref[:PIECE, :] = text[...]
        peer_ref[PIECE:, :] = text_c[...]

    @pl.when(core[0] == 1)
    def _():
        peer_ref[...] = image[...]
        first_ref[:PIECE, :] = text_c[...]
        first_ref[PIECE:, :] = text[...]


def scores_first(core, scale, *refs):
    a1, a2, b1 = refs[0:4], refs[4:8], refs[8:12]
    s_ref, x_ref, st_ref = refs[12:]
    me = core[0]
    for slot in range(4):
        at = slice(slot * CHIP, (slot + 1) * CHIP)
        x_ref[0, at, :] = b1[slot][...]

        @pl.when(me == 0)
        def _():
            x_ref[1, at, :] = a1[slot][...]

        @pl.when(me == 1)
        def _():
            x_ref[1, at, :] = a2[slot][...]

    st_ref[...] = jnp.ones((8, KIND), F32)
    col_max, col_sum = score_tiles(
        scale[0],
        lambda part: x_ref[1 - me, part, :],
        lambda part: x_ref[me, part, :],
        s_ref,
        st_ref,
        jnp.full((1, KIND), -1e30, F32),
        jnp.zeros((1, KIND), F32),
    )
    st_ref[4:5, :] = col_max
    st_ref[5:6, :] = col_sum
    total = jnp.zeros((1, 1), F32)
    for j in range(2):
        here = jnp.where(on_diagonal(j), s_ref[:TILE, j * 128 : (j + 1) * 128], 0.0)
        total += jnp.sum(jnp.sum(here, axis=0, keepdims=True), axis=1, keepdims=True)
    st_ref[6:7, :] = jnp.broadcast_to(total, (1, KIND))


def scores_second(core, scale, x_ref, st1, *refs):
    a2, text0, b2 = refs[0:4], refs[4], refs[5:8]
    s_ref, y_ref, st_ref, line = refs[8:]
    me = core[0]

    @pl.when(me == 0)
    def _():
        y_ref[0, :CHIP, :] = text0[...]
        for slot in range(4):
            y_ref[1, slot * CHIP : (slot + 1) * CHIP, :] = a2[slot][...]

    @pl.when(me == 1)
    def _():
        y_ref[0, :CHIP, :] = a2[0][...]

    for slot in range(1, 4):
        y_ref[0, slot * CHIP : (slot + 1) * CHIP, :] = b2[slot - 1][...]

    col_max, col_sum = score_tiles(
        scale[0],
        lambda part: y_ref[1 - me, part, :],
        lambda part: x_ref[me, part, :],
        s_ref,
        line,
        st1[4:5, :],
        st1[5:6, :],
    )
    st_ref[...] = jnp.concatenate(
        [st1[0:1, :], line[0:1, :], st1[1:2, :], line[1:2, :], col_max, col_sum, st1[6:8, :]], axis=0
    )


def join(a, b):
    top = jnp.maximum(a[0:2], b[0:2])
    total = a[2:4] * jnp.exp(a[0:2] - top) + b[2:4] * jnp.exp(b[0:2] - top)
    return jnp.concatenate([top, total, a[4:5] + b[4:5], jnp.ones((3, KIND), F32)], axis=0)


def join_cores(core, mine_ref, peer_ref, *refs):
    o_ref = refs[-1]
    a, b = mine_ref[...], peer_ref[...]
    rows = join(a[0:5], b[0:5])
    rows = jnp.concatenate([rows[0:4], a[6:7], rows[5:8]], axis=0)
    cols = jnp.concatenate([b[4:5], a[4:5], b[5:6], a[5:6], jnp.zeros((1, KIND), F32), rows[5:8]], axis=0)
    o_ref[...] = jnp.where(core[0] == 0, rows, cols)


def join_pair(a_ref, b_ref, *refs):
    o_ref = refs[-1]
    b = b_ref[...]
    o_ref[...] = join(a_ref[...], jnp.concatenate([b[1:2], b[0:1], b[3:4], b[2:3], b[4:8]], axis=0))


def join_ring(a_ref, b1_ref, b2_ref, b3_ref, *refs):
    out = a_ref[...]
    for k, b_ref in enumerate((b1_ref, b2_ref, b3_ref)):
        b, cut = b_ref[...], KIND - (k + 1) * CHIP
        out = join(out, jnp.concatenate([b[:, cut:], b[:, :cut]], axis=1))
    refs[-1][...] = jnp.concatenate([out[0:2] + jnp.log(out[2:4]), out[2:8]], axis=0)


def grad_weights(kind, core, s_ref, mine_ref, peer_ref, g_ref):
    image = core[0] == 0
    rows = jnp.where(image, mine_ref[kind : kind + 1, :], peer_ref[kind : kind + 1, :])
    cols = jnp.where(image, peer_ref[0:1, :], mine_ref[1:2, :])
    for r in range(2):
        lse = jnp.broadcast_to(rows[:, r * TILE : (r + 1) * TILE], (128, TILE)).T
        for j in range(KIND // 128):
            at = slice(j * 128, (j + 1) * 128)
            s = s_ref[r * TILE : (r + 1) * TILE, at]
            g = 0.5 * (jnp.exp(s - lse) + jnp.exp(s - cols[:, at]))
            if kind == 0 and r == 0 and j < 2:
                g = g - jnp.where(on_diagonal(j) & image, 1.0, 0.0)
            g_ref[r * TILE : (r + 1) * TILE, at] = g.astype(BF16)


def spread(value):
    high = value.astype(BF16).astype(F32)
    middle = (value - high).astype(BF16).astype(F32)
    low = value - high - middle
    lane = lax.broadcasted_iota(jnp.int32, (EXTRA, WIDTH), 1)
    out = jnp.where(lane < 128, high, jnp.where(lane < 256, middle, low))
    return out.astype(BF16)


def gathered(rows):
    rows = rows[0:1, :].astype(F32)
    return rows[:, 0:1] + rows[:, 128:129] + rows[:, 256:257]


def product(core, half, left, left_t, first, second, outs):
    at = slice(half * TILE, (half + 1) * TILE)

    def write(out, me):
        outs[0][0:CHIP, :] = out[:CHIP] if half == 0 else out[:CHIP].astype(BF16)
        if len(outs) == 3:
            outs[1 + me][...] = out[CHIP : CHIP + PIECE].astype(BF16)
            outs[2 - me][...] = out[CHIP + PIECE :].astype(BF16)
        else:
            outs[1][0:CHIP, :] = out[CHIP:].astype(BF16)

    @pl.when(core[0] == 0)
    def _():
        out = jnp.dot(left[0][at, :], first[0], preferred_element_type=F32)
        write(out + jnp.dot(left[1][at, :], second[0], preferred_element_type=F32), 0)

    @pl.when(core[0] == 1)
    def _():
        over = (((0,), (0,)), ((), ()))
        out = lax.dot_general(left_t[0][:, at], first[0], over, preferred_element_type=F32)
        write(out + lax.dot_general(left_t[1][:, at], second[0], over, preferred_element_type=F32), 1)


def grads_other(half, core, g1, g2, r2, x_ref, y_ref, mine_ref, peer_ref, *outs):
    product(core, half, (g2, r2), (g1, g2), x_ref, y_ref, outs[0:2])
    peer = peer_ref[...]
    term = jnp.sum(jnp.sum(peer[0:2], axis=0, keepdims=True), axis=1, keepdims=True)
    term = term - jnp.where(core[0] == 0, 0.0, 2.0 * peer[4:5, 0:1])
    if half == 0:
        outs[2][...] = jnp.broadcast_to(term, (8, 128))
    for out in outs[1 - half : 2]:
        out[CHIP:, :] = spread(term)


def grads_own(half, core, g1, r1, r2, x_ref, y_ref, *outs):
    product(core, half, (g1, r1), (r1, r2), x_ref, y_ref, outs)


def sum_other(core, acc, r1, r2, r3, term, *refs):
    same_ref, cross_ref, total_ref = refs[-3:]
    out = acc[...]
    total = term[0:1, 0:1]
    for r in (r1, r2, r3):
        out = out + r[0:CHIP, :].astype(F32)
        total = total + gathered(r[CHIP:, :])
    low, high = out[:PIECE].astype(BF16), out[PIECE:].astype(BF16)
    image = core[0] == 0
    same_ref[0:PIECE, :] = jnp.where(image, low, high)
    cross_ref[0:PIECE, :] = jnp.where(image, high, low)
    rows = spread(total)
    same_ref[PIECE:, :] = rows
    cross_ref[PIECE:, :] = rows
    total_ref[...] = jnp.broadcast_to(total, (8, 128))


def sum_own(core, acc, r2, r3, total, keep_ref, give_a_ref, give_b_ref):
    out = acc[...]
    for r in (r2, r3):
        out = out + r[...].astype(F32)
    low, high = out[:PIECE], out[PIECE:]
    image = core[0] == 0
    keep_ref[...] = jnp.where(image, low, high)
    give = jnp.where(image, high, low).astype(BF16)
    give_a_ref[0 : PIECE // 2, :] = give[: PIECE // 2]
    give_a_ref[PIECE // 2 :, :] = spread(total[0:1, 0:1])
    give_b_ref[...] = give[PIECE // 2 :]


def finish(core, scale, keep, got_a, got_b, same, cross, near_same, near_cross, total, image_ref, text_ref, loss_ref):
    mine = (scale[0] * (keep[...] + same[0:PIECE, :].astype(F32) + near_same[...].astype(F32))).astype(BF16)
    got = jnp.concatenate([got_a[: PIECE // 2, :], got_b[...]], axis=0)
    other = (scale[0] * (got.astype(F32) + cross[0:PIECE, :].astype(F32) + near_cross[...].astype(F32))).astype(BF16)
    image = core[0] == 0
    image_ref[...] = jnp.where(image, mine, other)
    text_ref[...] = jnp.where(image, other, mine)
    loss = total[0:1, 0:1] + gathered(got_a[PIECE // 2 :, :]) + gathered(same[PIECE:, :]) + gathered(cross[PIECE:, :])
    loss_ref[0] = loss[0, 0] / (16.0 * 2 * KIND)


def on_device(image, text, logit_scale):
    c = lax.axis_index("c")
    yl = lax.axis_index("yl")
    is_image = c == 0
    ring = jnp.where(is_image, lax.axis_index("x"), lax.axis_index("z"))
    core = c.reshape(1)
    odd = (ring & 1).reshape(1)
    mat = functools.partial(shape, dtype=BF16)

    chip = mat(CHIP, WIDTH)
    image_own = lax.dynamic_slice_in_dim(image, yl * CHIP, CHIP, 0)
    image_other = lax.dynamic_slice_in_dim(image, (1 - yl) * CHIP, CHIP, 0)
    image_own, image_other = lax.optimization_barrier((image_own, image_other))
    first, peer_first = call(prepare, (chip, chip), [SMEM] * 2 + [VMEM] * 3)(core, odd, image_own, text, move(text, FLIP_C))
    text_y = move(first, FLIP_YH)
    ring1 = [move(first, AHEAD[4 - slot]) for slot in (1, 2, 3)]
    second = jnp.where(is_image, image_other, text_y)
    ring2 = [move(second, AHEAD[3]), move(ring1[1], FLIP_Y), move(second, AHEAD[1])]
    ring1[0], ring1[1], ring1[2], ring2[1] = lax.optimization_barrier((*ring1, ring2[1]))
    peer1 = [move(v, FLIP_C) for v in ring1]
    text_yc = move(text_y, FLIP_C)
    peer2 = [move(v, FLIP_C) for v in ring2]

    half = 2 * KIND * KIND * WIDTH
    s1, x, st1 = call(
        scores_first,
        (shape(KIND, KIND), mat(2, KIND, WIDTH), shape(8, KIND)),
        [SMEM] * 2 + [VMEM] * 12,
        flops=half,
        bytes_accessed=KIND * KIND * 4,
    )(core, logit_scale, first, *ring1, second, *ring2, peer_first, *peer1)
    s2, y, st = call(
        scores_second,
        (shape(KIND, KIND), mat(2, KIND, WIDTH), shape(8, KIND)),
        [SMEM] * 2 + [VMEM] * 10,
        scratch=[pltpu.VMEM((8, KIND), F32)],
        flops=half,
        bytes_accessed=KIND * KIND * 4,
    )(core, logit_scale, x, st1, image_other, *ring2, text_yc, *peer2)

    stats = shape(8, KIND)
    held = (s1, s2, x, y)
    side = call(join_cores, stats, [SMEM] + [VMEM] * 6)(core, st, move(st, FLIP_C), *held)
    side = call(join_pair, stats, [VMEM] * 6)(side, move(side, FLIP_Y), *held)
    others = [move(side, AHEAD[4 - k]) for k in (1, 2, 3)]
    side = call(join_ring, stats, [VMEM] * 8)(side, *others, *held)
    peer = move(side, FLIP_C)

    weights = lambda kind, s: call(functools.partial(grad_weights, kind), mat(KIND, KIND), [SMEM] + [VMEM] * 3)(
        core, s, side, peer
    )
    g2 = weights(1, s2)
    r2 = move(g2, FLIP_C)
    g1 = weights(0, s1)
    r1 = move(g1, FLIP_C)
    long, own, small = mat(CHIP + EXTRA, WIDTH), shape(CHIP, WIDTH), shape(8, 128)

    def grads(body, out_shape, *operands):
        return call(body, out_shape, [SMEM] + [VMEM] * len(operands), flops=half)(core, *operands)

    send_2, send_3 = grads(functools.partial(grads_other, 1), (long, long), g1, g2, r2, x, y, side, peer)
    acc2, send_1, term = grads(functools.partial(grads_other, 0), (own, long, small), g1, g2, r2, x, y, side, peer)
    got2 = [move(v, AHEAD[k + 1]) for k, v in enumerate((send_1, send_2, send_3))]
    send_2, send_3 = grads(functools.partial(grads_own, 1), (chip, chip), g1, r1, r2, x, y)
    half_chip = mat(PIECE, WIDTH)
    acc1, near_same, near_cross = grads(functools.partial(grads_own, 0), (own, half_chip, half_chip), g1, r1, r2, x, y)
    near_same, near_cross = move(near_same, AHEAD[1]), move(near_cross, AHEAD_CROSS)
    got1 = [move(send_2, AHEAD[2]), move(send_3, AHEAD[3])]
    piece, part, tail = mat(PIECE, WIDTH), mat(PIECE // 2, WIDTH), mat(PIECE + EXTRA, WIDTH)
    same, cross, total = grads(sum_other, (tail, tail, small), acc2, *got2, term, send_2, acc1)
    same, cross = move(same, FLIP_Y), move(cross, CROSS_Y)
    keep, give_a, give_b = grads(
        sum_own, (shape(PIECE, WIDTH), mat(PIECE // 2 + EXTRA, WIDTH), part), acc1, *got1, total
    )
    grad_image, grad_text, loss = call(
        finish, (piece, piece, shape(1)), [SMEM] * 2 + [VMEM] * 8, out_specs=(VMEM, VMEM, SMEM)
    )(core, logit_scale, keep, move(give_a, FLIP_C), move(give_b, FLIP_C), same, cross, near_same, near_cross, total)
    return loss, grad_image, grad_text


def solution(mesh):
    fine = Mesh(mesh.devices.reshape(SIZES), AXES)
    every = P(AXES, None)
    return jax.shard_map(
        on_device,
        mesh=fine,
        in_specs=(P(("x", "z", "yh"), None), every, P()),
        out_specs=(P(), every, every),
        check_vma=False,
    )
```

```python
import functools
import math

import jax
import jax.numpy as jnp
from jax import lax
from jax.experimental import pallas as pl
from jax.experimental.pallas import tpu as pltpu
from jax.sharding import Mesh, PartitionSpec as P

AXES = ("x", "z", "yh", "yl", "c")
SIZES = (4, 4, 2, 2, 2)
PIECE = 96
CHIP = 2 * PIECE
KIND = 4 * CHIP
TILE = KIND // 2
WIDTH = 1024
LOG2_E = 1.0 / math.log(2.0)
EXTRA = 16
VMEM_LIMIT = 16 * 1024 * 1024

F32 = jnp.float32
BF16 = jnp.bfloat16
VMEM = pl.BlockSpec(memory_space=pltpu.VMEM)
SMEM = pl.BlockSpec(memory_space=pltpu.SMEM)


def pairs_of(move):
    def index(x, z, yh, yl, c):
        return (((x * 4 + z) * 2 + yh) * 2 + yl) * 2 + c

    return [
        (index(x, z, yh, yl, c), index(*move(x, z, yh, yl, c)))
        for x in range(4) for z in range(4) for yh in range(2) for yl in range(2) for c in range(2)
    ]


def on_ring(turn):
    return lambda x, z, yh, yl, c: (turn(x), z, yh, yl, c) if c == 0 else (x, turn(z), yh, yl, c)


AHEAD = [pairs_of(on_ring(lambda r, d=d: (r + d) % 4)) for d in range(4)]
ahead_one = on_ring(lambda r: (r + 1) % 4)
AHEAD_CROSS = pairs_of(lambda x, z, yh, yl, c: (*ahead_one(x, z, yh, yl, c)[:4], 1 - c))
flip_y = lambda x, z, yh, yl, c: (x, z, yh, 1 - yl, c) if c == 0 else (x, z, 1 - yh, 1 - yl, c)
FLIP_Y = pairs_of(flip_y)
CROSS_Y = pairs_of(lambda x, z, yh, yl, c: (*flip_y(x, z, yh, yl, c)[:4], 1 - c))
FLIP_YH = [(a, b) for a, b in FLIP_Y if a % 2 == 1]
FLIP_C = pairs_of(lambda x, z, yh, yl, c: (x, z, yh, yl, 1 - c))


def move(value, pairs):
    return lax.ppermute(value, AXES, pairs)


def call(body, out_shape, specs, scratch=(), flops=0, bytes_accessed=0, out_specs=None):
    return pl.pallas_call(
        body,
        out_shape=out_shape,
        in_specs=specs,
        out_specs=out_specs or jax.tree.map(lambda _: VMEM, out_shape),
        scratch_shapes=list(scratch),
        compiler_params=pltpu.CompilerParams(vmem_limit_bytes=VMEM_LIMIT),
        cost_estimate=pl.CostEstimate(flops=flops, bytes_accessed=bytes_accessed, transcendentals=0),
    )


def shape(*dims, dtype=F32):
    return jax.ShapeDtypeStruct(dims, dtype)


def lanes_of(s, combine):
    part = s[:, :128]
    for j in range(1, KIND // 128):
        part = combine(part, s[:, j * 128 : (j + 1) * 128])
    return part


def on_diagonal(j):
    row = lax.broadcasted_iota(jnp.int32, (TILE, 128), 0)
    return (row == lax.broadcasted_iota(jnp.int32, (TILE, 128), 1) + j * 128) & (row < CHIP)


def score_tiles(factor, rows, cols, s_ref, row_ref, col_max, col_sum):
    for r in range(3):
        part = slice(r * 256, (r + 1) * 256)
        s = factor * lax.dot_general(rows(part), cols(slice(None)), (((1,), (1,)), ((), ())), preferred_element_type=F32)
        s_ref[part, :] = s
        top = lanes_of(s, jnp.maximum)
        row_ref[0:1, part] = jnp.max(top.T, axis=0, keepdims=True)
        e = jnp.exp2(s - jnp.max(top, axis=1, keepdims=True))
        row_ref[1:2, part] = jnp.sum(lanes_of(e, jnp.add).T, axis=0, keepdims=True)
        new_max = jnp.maximum(col_max, jnp.max(s, axis=0, keepdims=True))
        col_sum = col_sum * jnp.exp2(col_max - new_max) + jnp.sum(jnp.exp2(s - new_max), axis=0, keepdims=True)
        col_max = new_max
    return col_max, col_sum


def prepare(core, odd, image, text, text_c, first_ref, peer_ref):
    @pl.when(core[0] == 0)
    def _():
        first_ref[...] = image[...]
        peer_ref[:PIECE, :] = text[...]
        peer_ref[PIECE:, :] = text_c[...]

    @pl.when(core[0] == 1)
    def _():
        peer_ref[...] = image[...]
        first_ref[:PIECE, :] = text_c[...]
        first_ref[PIECE:, :] = text[...]


def scores_first(core, scale, *refs):
    a1, a2, b1 = refs[0:4], refs[4:8], refs[8:12]
    s_ref, x_ref, st_ref = refs[12:]
    me = core[0]
    for slot in range(4):
        at = slice(slot * CHIP, (slot + 1) * CHIP)
        x_ref[0, at, :] = b1[slot][...]

        @pl.when(me == 0)
        def _():
            x_ref[1, at, :] = a1[slot][...]

        @pl.when(me == 1)
        def _():
            x_ref[1, at, :] = a2[slot][...]

    st_ref[...] = jnp.ones((8, KIND), F32)
    col_max, col_sum = score_tiles(
        scale[0] * LOG2_E,
        lambda part: x_ref[1 - me, part, :],
        lambda part: x_ref[me, part, :],
        s_ref,
        st_ref,
        jnp.full((1, KIND), -1e30, F32),
        jnp.zeros((1, KIND), F32),
    )
    st_ref[4:5, :] = col_max
    st_ref[5:6, :] = col_sum
    total = jnp.zeros((1, 1), F32)
    for j in range(2):
        here = jnp.where(on_diagonal(j), s_ref[:TILE, j * 128 : (j + 1) * 128], 0.0)
        total += jnp.sum(jnp.sum(here, axis=0, keepdims=True), axis=1, keepdims=True)
    st_ref[6:7, :] = jnp.broadcast_to(total, (1, KIND))


def scores_second(core, scale, x_ref, st1, *refs):
    a2, text0, b2 = refs[0:4], refs[4], refs[5:8]
    s_ref, y_ref, st_ref, line = refs[8:]
    me = core[0]

    @pl.when(me == 0)
    def _():
        y_ref[0, :CHIP, :] = text0[...]
        for slot in range(4):
            y_ref[1, slot * CHIP : (slot + 1) * CHIP, :] = a2[slot][...]

    @pl.when(me == 1)
    def _():
        y_ref[0, :CHIP, :] = a2[0][...]

    for slot in range(1, 4):
        y_ref[0, slot * CHIP : (slot + 1) * CHIP, :] = b2[slot - 1][...]

    col_max, col_sum = score_tiles(
        scale[0] * LOG2_E,
        lambda part: y_ref[1 - me, part, :],
        lambda part: x_ref[me, part, :],
        s_ref,
        line,
        st1[4:5, :],
        st1[5:6, :],
    )
    st_ref[...] = jnp.concatenate(
        [st1[0:1, :], line[0:1, :], st1[1:2, :], line[1:2, :], col_max, col_sum, st1[6:8, :]], axis=0
    )


def join(a, b):
    top = jnp.maximum(a[0:2], b[0:2])
    total = a[2:4] * jnp.exp2(a[0:2] - top) + b[2:4] * jnp.exp2(b[0:2] - top)
    return jnp.concatenate([top, total, a[4:5] + b[4:5], jnp.ones((3, KIND), F32)], axis=0)


def join_cores(core, mine_ref, peer_ref, *refs):
    o_ref = refs[-1]
    a, b = mine_ref[...], peer_ref[...]
    rows = join(a[0:5], b[0:5])
    rows = jnp.concatenate([rows[0:4], a[6:7], rows[5:8]], axis=0)
    cols = jnp.concatenate([b[4:5], a[4:5], b[5:6], a[5:6], jnp.zeros((1, KIND), F32), rows[5:8]], axis=0)
    o_ref[...] = jnp.where(core[0] == 0, rows, cols)


def join_pair(a_ref, b_ref, *refs):
    o_ref = refs[-1]
    b = b_ref[...]
    o_ref[...] = join(a_ref[...], jnp.concatenate([b[1:2], b[0:1], b[3:4], b[2:3], b[4:8]], axis=0))


def join_ring(a_ref, b1_ref, b2_ref, b3_ref, *refs):
    out = a_ref[...]
    for k, b_ref in enumerate((b1_ref, b2_ref, b3_ref)):
        b, cut = b_ref[...], KIND - (k + 1) * CHIP
        out = join(out, jnp.concatenate([b[:, cut:], b[:, :cut]], axis=1))
    refs[-1][...] = jnp.concatenate([out[0:2] + jnp.log2(out[2:4]), out[2:8]], axis=0)


def grad_weights(kind, core, s_ref, mine_ref, peer_ref, g_ref):
    image = core[0] == 0
    rows = jnp.where(image, mine_ref[kind : kind + 1, :], peer_ref[kind : kind + 1, :])
    cols = jnp.where(image, peer_ref[0:1, :], mine_ref[1:2, :])
    for r in range(2):
        lse = jnp.broadcast_to(rows[:, r * TILE : (r + 1) * TILE], (128, TILE)).T
        for j in range(KIND // 128):
            at = slice(j * 128, (j + 1) * 128)
            s = s_ref[r * TILE : (r + 1) * TILE, at]
            g = 0.5 * (jnp.exp2(s - lse) + jnp.exp2(s - cols[:, at]))
            if kind == 0 and r == 0 and j < 2:
                g = g - jnp.where(on_diagonal(j) & image, 1.0, 0.0)
            g_ref[r * TILE : (r + 1) * TILE, at] = g.astype(BF16)


def spread(value):
    high = value.astype(BF16).astype(F32)
    middle = (value - high).astype(BF16).astype(F32)
    low = value - high - middle
    lane = lax.broadcasted_iota(jnp.int32, (EXTRA, WIDTH), 1)
    out = jnp.where(lane < 128, high, jnp.where(lane < 256, middle, low))
    return out.astype(BF16)


def gathered(rows):
    rows = rows[0:1, :].astype(F32)
    return rows[:, 0:1] + rows[:, 128:129] + rows[:, 256:257]


def product(core, half, left, left_t, first, second, outs):
    at = slice(half * TILE, (half + 1) * TILE)

    def write(out, me):
        outs[0][0:CHIP, :] = out[:CHIP] if half == 0 else out[:CHIP].astype(BF16)
        if len(outs) == 3:
            outs[1 + me][...] = out[CHIP : CHIP + PIECE].astype(BF16)
            outs[2 - me][...] = out[CHIP + PIECE :].astype(BF16)
        else:
            outs[1][0:CHIP, :] = out[CHIP:].astype(BF16)

    @pl.when(core[0] == 0)
    def _():
        out = jnp.dot(left[0][at, :], first[0], preferred_element_type=F32)
        write(out + jnp.dot(left[1][at, :], second[0], preferred_element_type=F32), 0)

    @pl.when(core[0] == 1)
    def _():
        over = (((0,), (0,)), ((), ()))
        out = lax.dot_general(left_t[0][:, at], first[0], over, preferred_element_type=F32)
        write(out + lax.dot_general(left_t[1][:, at], second[0], over, preferred_element_type=F32), 1)


def grads_other(half, core, g1, g2, r2, x_ref, y_ref, mine_ref, peer_ref, *outs):
    product(core, half, (g2, r2), (g1, g2), x_ref, y_ref, outs[0:2])
    peer = peer_ref[...]
    term = jnp.sum(jnp.sum(peer[0:2], axis=0, keepdims=True), axis=1, keepdims=True)
    term = term - jnp.where(core[0] == 0, 0.0, 2.0 * peer[4:5, 0:1])
    if half == 0:
        outs[2][...] = jnp.broadcast_to(term, (8, 128))
    for out in outs[1 - half : 2]:
        out[CHIP:, :] = spread(term)


def grads_own(half, core, g1, r1, r2, x_ref, y_ref, *outs):
    product(core, half, (g1, r1), (r1, r2), x_ref, y_ref, outs)


def sum_other(core, acc, r1, r2, r3, term, *refs):
    same_ref, cross_ref, total_ref = refs[-3:]
    out = acc[...]
    total = term[0:1, 0:1]
    for r in (r1, r2, r3):
        out = out + r[0:CHIP, :].astype(F32)
        total = total + gathered(r[CHIP:, :])
    low, high = out[:PIECE].astype(BF16), out[PIECE:].astype(BF16)
    image = core[0] == 0
    same_ref[0:PIECE, :] = jnp.where(image, low, high)
    cross_ref[0:PIECE, :] = jnp.where(image, high, low)
    rows = spread(total)
    same_ref[PIECE:, :] = rows
    cross_ref[PIECE:, :] = rows
    total_ref[...] = jnp.broadcast_to(total, (8, 128))


def sum_own(core, acc, r2, r3, total, keep_ref, give_a_ref, give_b_ref):
    out = acc[...]
    for r in (r2, r3):
        out = out + r[...].astype(F32)
    low, high = out[:PIECE], out[PIECE:]
    image = core[0] == 0
    keep_ref[...] = jnp.where(image, low, high)
    give = jnp.where(image, high, low).astype(BF16)
    give_a_ref[0 : PIECE // 2, :] = give[: PIECE // 2]
    give_a_ref[PIECE // 2 :, :] = spread(total[0:1, 0:1])
    give_b_ref[...] = give[PIECE // 2 :]


def finish(core, scale, keep, got_a, got_b, same, cross, near_same, near_cross, total, image_ref, text_ref, loss_ref):
    mine = (scale[0] * (keep[...] + same[0:PIECE, :].astype(F32) + near_same[...].astype(F32))).astype(BF16)
    got = jnp.concatenate([got_a[: PIECE // 2, :], got_b[...]], axis=0)
    other = (scale[0] * (got.astype(F32) + cross[0:PIECE, :].astype(F32) + near_cross[...].astype(F32))).astype(BF16)
    image = core[0] == 0
    image_ref[...] = jnp.where(image, mine, other)
    text_ref[...] = jnp.where(image, other, mine)
    loss = total[0:1, 0:1] + gathered(got_a[PIECE // 2 :, :]) + gathered(same[PIECE:, :]) + gathered(cross[PIECE:, :])
    loss_ref[0] = loss[0, 0] * (math.log(2.0) / (16.0 * 2 * KIND))


def on_device(image, text, logit_scale):
    c = lax.axis_index("c")
    yl = lax.axis_index("yl")
    is_image = c == 0
    ring = jnp.where(is_image, lax.axis_index("x"), lax.axis_index("z"))
    core = c.reshape(1)
    odd = (ring & 1).reshape(1)
    mat = functools.partial(shape, dtype=BF16)

    chip = mat(CHIP, WIDTH)
    image_own = lax.dynamic_slice_in_dim(image, yl * CHIP, CHIP, 0)
    image_other = lax.dynamic_slice_in_dim(image, (1 - yl) * CHIP, CHIP, 0)
    image_own, image_other = lax.optimization_barrier((image_own, image_other))
    first, peer_first = call(prepare, (chip, chip), [SMEM] * 2 + [VMEM] * 3)(core, odd, image_own, text, move(text, FLIP_C))
    text_y = move(first, FLIP_YH)
    ring1 = [move(first, AHEAD[4 - slot]) for slot in (1, 2, 3)]
    second = jnp.where(is_image, image_other, text_y)
    ring2 = [move(second, AHEAD[3]), move(ring1[1], FLIP_Y), move(second, AHEAD[1])]
    ring1[0], ring1[1], ring1[2], ring2[1] = lax.optimization_barrier((*ring1, ring2[1]))
    peer1 = [move(v, FLIP_C) for v in ring1]
    text_yc = move(text_y, FLIP_C)
    peer2 = [move(v, FLIP_C) for v in ring2]

    half = 2 * KIND * KIND * WIDTH
    s1, x, st1 = call(
        scores_first,
        (shape(KIND, KIND), mat(2, KIND, WIDTH), shape(8, KIND)),
        [SMEM] * 2 + [VMEM] * 12,
        flops=half,
        bytes_accessed=KIND * KIND * 4,
    )(core, logit_scale, first, *ring1, second, *ring2, peer_first, *peer1)
    s2, y, st = call(
        scores_second,
        (shape(KIND, KIND), mat(2, KIND, WIDTH), shape(8, KIND)),
        [SMEM] * 2 + [VMEM] * 10,
        scratch=[pltpu.VMEM((8, KIND), F32)],
        flops=half,
        bytes_accessed=KIND * KIND * 4,
    )(core, logit_scale, x, st1, image_other, *ring2, text_yc, *peer2)

    stats = shape(8, KIND)
    held = (s1, s2, x, y)
    side = call(join_cores, stats, [SMEM] + [VMEM] * 6)(core, st, move(st, FLIP_C), *held)
    side = call(join_pair, stats, [VMEM] * 6)(side, move(side, FLIP_Y), *held)
    others = [move(side, AHEAD[4 - k]) for k in (1, 2, 3)]
    side = call(join_ring, stats, [VMEM] * 8)(side, *others, *held)
    peer = move(side, FLIP_C)

    weights = lambda kind, s: call(functools.partial(grad_weights, kind), mat(KIND, KIND), [SMEM] + [VMEM] * 3)(
        core, s, side, peer
    )
    g2 = weights(1, s2)
    r2 = move(g2, FLIP_C)
    g1 = weights(0, s1)
    r1 = move(g1, FLIP_C)
    long, own, small = mat(CHIP + EXTRA, WIDTH), shape(CHIP, WIDTH), shape(8, 128)

    def grads(body, out_shape, *operands):
        return call(body, out_shape, [SMEM] + [VMEM] * len(operands), flops=half)(core, *operands)

    send_2, send_3 = grads(functools.partial(grads_other, 1), (long, long), g1, g2, r2, x, y, side, peer)
    acc2, send_1, term = grads(functools.partial(grads_other, 0), (own, long, small), g1, g2, r2, x, y, side, peer)
    got2 = [move(v, AHEAD[k + 1]) for k, v in enumerate((send_1, send_2, send_3))]
    send_2, send_3 = grads(functools.partial(grads_own, 1), (chip, chip), g1, r1, r2, x, y)
    half_chip = mat(PIECE, WIDTH)
    acc1, near_same, near_cross = grads(functools.partial(grads_own, 0), (own, half_chip, half_chip), g1, r1, r2, x, y)
    near_same, near_cross = move(near_same, AHEAD[1]), move(near_cross, AHEAD_CROSS)
    got1 = [move(send_2, AHEAD[2]), move(send_3, AHEAD[3])]
    piece, part, tail = mat(PIECE, WIDTH), mat(PIECE // 2, WIDTH), mat(PIECE + EXTRA, WIDTH)
    same, cross, total = grads(sum_other, (tail, tail, small), acc2, *got2, term, send_2, acc1)
    same, cross = move(same, FLIP_Y), move(cross, CROSS_Y)
    keep, give_a, give_b = grads(
        sum_own, (shape(PIECE, WIDTH), mat(PIECE // 2 + EXTRA, WIDTH), part), acc1, *got1, total
    )
    grad_image, grad_text, loss = call(
        finish, (piece, piece, shape(1)), [SMEM] * 2 + [VMEM] * 8, out_specs=(VMEM, VMEM, SMEM)
    )(core, logit_scale, keep, move(give_a, FLIP_C), move(give_b, FLIP_C), same, cross, near_same, near_cross, total)
    return loss, grad_image, grad_text


def solution(mesh):
    fine = Mesh(mesh.devices.reshape(SIZES), AXES)
    every = P(AXES, None)
    return jax.shard_map(
        on_device,
        mesh=fine,
        in_specs=(P(("x", "z", "yh"), None), every, P()),
        out_specs=(P(), every, every),
        check_vma=False,
    )
```

```python
import functools
import math

import jax
import jax.numpy as jnp
from jax import lax
from jax.experimental import pallas as pl
from jax.experimental.pallas import tpu as pltpu
from jax.sharding import Mesh, PartitionSpec as P

AXES = ("x", "z", "yh", "yl", "c")
SIZES = (4, 4, 2, 2, 2)
PIECE = 96
CHIP = 2 * PIECE
KIND = 4 * CHIP
TILE = KIND // 2
WIDTH = 1024
LOG2_E = 1.0 / math.log(2.0)
EXTRA = 16
VMEM_LIMIT = 16 * 1024 * 1024

F32 = jnp.float32
BF16 = jnp.bfloat16
VMEM = pl.BlockSpec(memory_space=pltpu.VMEM)
SMEM = pl.BlockSpec(memory_space=pltpu.SMEM)


def pairs_of(move):
    def index(x, z, yh, yl, c):
        return (((x * 4 + z) * 2 + yh) * 2 + yl) * 2 + c

    return [
        (index(x, z, yh, yl, c), index(*move(x, z, yh, yl, c)))
        for x in range(4) for z in range(4) for yh in range(2) for yl in range(2) for c in range(2)
    ]


def on_ring(turn):
    return lambda x, z, yh, yl, c: (turn(x), z, yh, yl, c) if c == 0 else (x, turn(z), yh, yl, c)


AHEAD = [pairs_of(on_ring(lambda r, d=d: (r + d) % 4)) for d in range(4)]
ahead_one = on_ring(lambda r: (r + 1) % 4)
AHEAD_CROSS = pairs_of(lambda x, z, yh, yl, c: (*ahead_one(x, z, yh, yl, c)[:4], 1 - c))
flip_y = lambda x, z, yh, yl, c: (x, z, yh, 1 - yl, c) if c == 0 else (x, z, 1 - yh, 1 - yl, c)
FLIP_Y = pairs_of(flip_y)
CROSS_Y = pairs_of(lambda x, z, yh, yl, c: (*flip_y(x, z, yh, yl, c)[:4], 1 - c))
FLIP_YH = [(a, b) for a, b in FLIP_Y if a % 2 == 1]
FLIP_C = pairs_of(lambda x, z, yh, yl, c: (x, z, yh, yl, 1 - c))


def move(value, pairs):
    return lax.ppermute(value, AXES, pairs)


def call(body, out_shape, specs, scratch=(), flops=0, bytes_accessed=0, out_specs=None):
    return pl.pallas_call(
        body,
        out_shape=out_shape,
        in_specs=specs,
        out_specs=out_specs or jax.tree.map(lambda _: VMEM, out_shape),
        scratch_shapes=list(scratch),
        compiler_params=pltpu.CompilerParams(vmem_limit_bytes=VMEM_LIMIT),
        cost_estimate=pl.CostEstimate(flops=flops, bytes_accessed=bytes_accessed, transcendentals=0),
    )


def shape(*dims, dtype=F32):
    return jax.ShapeDtypeStruct(dims, dtype)


def lanes_of(s, combine):
    part = s[:, :128]
    for j in range(1, KIND // 128):
        part = combine(part, s[:, j * 128 : (j + 1) * 128])
    return part


def on_diagonal(j):
    row = lax.broadcasted_iota(jnp.int32, (TILE, 128), 0)
    return (row == lax.broadcasted_iota(jnp.int32, (TILE, 128), 1) + j * 128) & (row < CHIP)


def score_tiles(factor, rows, cols, s_ref, row_ref, col_max, col_sum):
    for r in range(3):
        part = slice(r * 256, (r + 1) * 256)
        s = factor * lax.dot_general(rows(part), cols(slice(None)), (((1,), (1,)), ((), ())), preferred_element_type=F32)
        s_ref[part, :] = s
        top = lanes_of(s, jnp.maximum)
        row_ref[0:1, part] = jnp.max(top.T, axis=0, keepdims=True)
        e = jnp.exp2(s - jnp.max(top, axis=1, keepdims=True))
        row_ref[1:2, part] = jnp.sum(lanes_of(e, jnp.add).T, axis=0, keepdims=True)
        new_max = jnp.maximum(col_max, jnp.max(s, axis=0, keepdims=True))
        col_sum = col_sum * jnp.exp2(col_max - new_max) + jnp.sum(jnp.exp2(s - new_max), axis=0, keepdims=True)
        col_max = new_max
    return col_max, col_sum


def prepare(core, odd, image, text, text_c, first_ref, peer_ref):
    @pl.when(core[0] == 0)
    def _():
        first_ref[...] = image[...]
        peer_ref[:PIECE, :] = text[...]
        peer_ref[PIECE:, :] = text_c[...]

    @pl.when(core[0] == 1)
    def _():
        peer_ref[...] = image[...]
        first_ref[:PIECE, :] = text_c[...]
        first_ref[PIECE:, :] = text[...]


def scores_first(core, scale, *refs):
    a1, a2, b1 = refs[0:4], refs[4:8], refs[8:12]
    s_ref, x_ref, st_ref = refs[12:]
    me = core[0]
    for slot in range(4):
        at = slice(slot * CHIP, (slot + 1) * CHIP)
        x_ref[0, at, :] = b1[slot][...]

        @pl.when(me == 0)
        def _():
            x_ref[1, at, :] = a1[slot][...]

        @pl.when(me == 1)
        def _():
            x_ref[1, at, :] = a2[slot][...]

    st_ref[...] = jnp.ones((8, KIND), F32)
    col_max, col_sum = score_tiles(
        scale[0] * LOG2_E,
        lambda part: x_ref[1 - me, part, :],
        lambda part: x_ref[me, part, :],
        s_ref,
        st_ref,
        jnp.full((1, KIND), -1e30, F32),
        jnp.zeros((1, KIND), F32),
    )
    st_ref[4:5, :] = col_max
    st_ref[5:6, :] = col_sum
    total = jnp.zeros((1, 1), F32)
    for j in range(2):
        here = jnp.where(on_diagonal(j), s_ref[:TILE, j * 128 : (j + 1) * 128], 0.0)
        total += jnp.sum(jnp.sum(here, axis=0, keepdims=True), axis=1, keepdims=True)
    st_ref[6:7, :] = jnp.broadcast_to(total, (1, KIND))


def scores_second(core, scale, x_ref, st1, *refs):
    a2, text0, b2 = refs[0:4], refs[4], refs[5:8]
    s_ref, y_ref, st_ref, line = refs[8:]
    me = core[0]

    @pl.when(me == 0)
    def _():
        y_ref[0, :CHIP, :] = text0[...]
        for slot in range(4):
            y_ref[1, slot * CHIP : (slot + 1) * CHIP, :] = a2[slot][...]

    @pl.when(me == 1)
    def _():
        y_ref[0, :CHIP, :] = a2[0][...]

    for slot in range(1, 4):
        y_ref[0, slot * CHIP : (slot + 1) * CHIP, :] = b2[slot - 1][...]

    col_max, col_sum = score_tiles(
        scale[0] * LOG2_E,
        lambda part: y_ref[1 - me, part, :],
        lambda part: x_ref[me, part, :],
        s_ref,
        line,
        st1[4:5, :],
        st1[5:6, :],
    )
    st_ref[...] = jnp.concatenate(
        [st1[0:1, :], line[0:1, :], st1[1:2, :], line[1:2, :], col_max, col_sum, st1[6:8, :]], axis=0
    )


def join(a, b):
    top = jnp.maximum(a[0:2], b[0:2])
    total = a[2:4] * jnp.exp2(a[0:2] - top) + b[2:4] * jnp.exp2(b[0:2] - top)
    return jnp.concatenate([top, total, a[4:5] + b[4:5], jnp.ones((3, KIND), F32)], axis=0)


def join_cores(core, mine_ref, peer_ref, *refs):
    o_ref = refs[-1]
    a, b = mine_ref[...], peer_ref[...]
    rows = join(a[0:5], b[0:5])
    rows = jnp.concatenate([rows[0:4], a[6:7], rows[5:8]], axis=0)
    cols = jnp.concatenate([b[4:5], a[4:5], b[5:6], a[5:6], jnp.zeros((1, KIND), F32), rows[5:8]], axis=0)
    o_ref[...] = jnp.where(core[0] == 0, rows, cols)


def join_pair(a_ref, b_ref, *refs):
    o_ref = refs[-1]
    b = b_ref[...]
    o_ref[...] = join(a_ref[...], jnp.concatenate([b[1:2], b[0:1], b[3:4], b[2:3], b[4:8]], axis=0))


def join_ring(a_ref, b1_ref, b2_ref, b3_ref, *refs):
    out = a_ref[...]
    for k, b_ref in enumerate((b1_ref, b2_ref, b3_ref)):
        b, cut = b_ref[...], KIND - (k + 1) * CHIP
        out = join(out, jnp.concatenate([b[:, cut:], b[:, :cut]], axis=1))
    refs[-1][...] = jnp.concatenate([out[0:2] + jnp.log2(out[2:4]), out[2:8]], axis=0)


def grad_weights(kind, core, s_ref, mine_ref, peer_ref, g_ref):
    image = core[0] == 0
    rows = jnp.where(image, mine_ref[kind : kind + 1, :], peer_ref[kind : kind + 1, :])
    cols = jnp.where(image, peer_ref[0:1, :], mine_ref[1:2, :])
    for r in range(2):
        lse = jnp.broadcast_to(rows[:, r * TILE : (r + 1) * TILE], (128, TILE)).T
        for j in range(KIND // 128):
            at = slice(j * 128, (j + 1) * 128)
            s = s_ref[r * TILE : (r + 1) * TILE, at]
            g = 0.5 * (jnp.exp2(s - lse) + jnp.exp2(s - cols[:, at]))
            if kind == 0 and r == 0 and j < 2:
                g = g - jnp.where(on_diagonal(j) & image, 1.0, 0.0)
            g_ref[r * TILE : (r + 1) * TILE, at] = g.astype(BF16)


def spread(value):
    high = value.astype(BF16).astype(F32)
    middle = (value - high).astype(BF16).astype(F32)
    low = value - high - middle
    lane = lax.broadcasted_iota(jnp.int32, (EXTRA, WIDTH), 1)
    out = jnp.where(lane < 128, high, jnp.where(lane < 256, middle, low))
    return out.astype(BF16)


def gathered(rows):
    rows = rows[0:1, :].astype(F32)
    return rows[:, 0:1] + rows[:, 128:129] + rows[:, 256:257]


def product(core, half, left, left_t, first, second, outs):
    at = slice(half * TILE, (half + 1) * TILE)

    def write(out, me):
        outs[0][0:CHIP, :] = out[:CHIP] if half == 0 else out[:CHIP].astype(BF16)
        if len(outs) == 3:
            outs[1 + me][...] = out[CHIP : CHIP + PIECE].astype(BF16)
            outs[2 - me][...] = out[CHIP + PIECE :].astype(BF16)
        else:
            outs[1][0:CHIP, :] = out[CHIP:].astype(BF16)

    @pl.when(core[0] == 0)
    def _():
        out = jnp.dot(left[0][at, :], first[0], preferred_element_type=F32)
        write(out + jnp.dot(left[1][at, :], second[0], preferred_element_type=F32), 0)

    @pl.when(core[0] == 1)
    def _():
        over = (((0,), (0,)), ((), ()))
        out = lax.dot_general(left_t[0][:, at], first[0], over, preferred_element_type=F32)
        write(out + lax.dot_general(left_t[1][:, at], second[0], over, preferred_element_type=F32), 1)


def grads_other(half, core, g1, g2, r2, x_ref, y_ref, mine_ref, peer_ref, *outs):
    product(core, half, (g2, r2), (g1, g2), x_ref, y_ref, outs[0:2])
    peer = peer_ref[...]
    term = jnp.sum(jnp.sum(peer[0:2], axis=0, keepdims=True), axis=1, keepdims=True)
    term = term - jnp.where(core[0] == 0, 0.0, 2.0 * peer[4:5, 0:1])
    if half == 0:
        outs[2][...] = jnp.broadcast_to(term, (8, 128))
    for out in outs[1 - half : 2]:
        out[CHIP:, :] = spread(term)


def grads_own(half, core, g1, r1, r2, x_ref, y_ref, *outs):
    product(core, half, (g1, r1), (r1, r2), x_ref, y_ref, outs)


def sum_other(core, acc, r1, r2, r3, term, *refs):
    same_ref, cross_ref, total_ref = refs[-3:]
    out = acc[...]
    total = term[0:1, 0:1]
    for r in (r1, r2, r3):
        out = out + r[0:CHIP, :].astype(F32)
        total = total + gathered(r[CHIP:, :])
    low, high = out[:PIECE].astype(BF16), out[PIECE:].astype(BF16)
    image = core[0] == 0
    same_ref[0:PIECE, :] = jnp.where(image, low, high)
    cross_ref[0:PIECE, :] = jnp.where(image, high, low)
    rows = spread(total)
    same_ref[PIECE:, :] = rows
    cross_ref[PIECE:, :] = rows
    total_ref[...] = jnp.broadcast_to(total, (8, 128))


def sum_own(core, acc, r2, r3, total, keep_ref, give_a_ref, give_b_ref):
    out = acc[...]
    for r in (r2, r3):
        out = out + r[...].astype(F32)
    low, high = out[:PIECE], out[PIECE:]
    image = core[0] == 0
    keep_ref[...] = jnp.where(image, low, high)
    give = jnp.where(image, high, low).astype(BF16)
    give_a_ref[0 : PIECE // 2, :] = give[: PIECE // 2]
    give_a_ref[PIECE // 2 :, :] = spread(total[0:1, 0:1])
    give_b_ref[...] = give[PIECE // 2 :]


def finish(core, scale, keep, got_a, got_b, same, cross, near_same, near_cross, total, image_ref, text_ref, loss_ref):
    mine = (scale[0] * (keep[...] + same[0:PIECE, :].astype(F32) + near_same[...].astype(F32))).astype(BF16)
    got = jnp.concatenate([got_a[: PIECE // 2, :], got_b[...]], axis=0)
    other = (scale[0] * (got.astype(F32) + cross[0:PIECE, :].astype(F32) + near_cross[...].astype(F32))).astype(BF16)
    image = core[0] == 0
    image_ref[...] = jnp.where(image, mine, other)
    text_ref[...] = jnp.where(image, other, mine)
    loss = total[0:1, 0:1] + gathered(got_a[PIECE // 2 :, :]) + gathered(same[PIECE:, :]) + gathered(cross[PIECE:, :])
    loss_ref[0] = loss[0, 0] * (math.log(2.0) / (16.0 * 2 * KIND))


def on_device(image, text, logit_scale):
    c = lax.axis_index("c")
    yl = lax.axis_index("yl")
    is_image = c == 0
    ring = jnp.where(is_image, lax.axis_index("x"), lax.axis_index("z"))
    core = c.reshape(1)
    odd = (ring & 1).reshape(1)
    mat = functools.partial(shape, dtype=BF16)

    chip = mat(CHIP, WIDTH)
    image_own = lax.dynamic_slice_in_dim(image, yl * CHIP, CHIP, 0)
    image_other = lax.dynamic_slice_in_dim(image, (1 - yl) * CHIP, CHIP, 0)
    image_own, image_other = lax.optimization_barrier((image_own, image_other))
    first, peer_first = call(prepare, (chip, chip), [SMEM] * 2 + [VMEM] * 3)(core, odd, image_own, text, move(text, FLIP_C))
    text_y = move(first, FLIP_YH)
    ring1 = [move(first, AHEAD[4 - slot]) for slot in (1, 2, 3)]
    second = jnp.where(is_image, image_other, text_y)
    ring2 = [move(second, AHEAD[3]), move(ring1[1], FLIP_Y), move(second, AHEAD[1])]
    ring1[0], ring1[1], ring1[2], ring2[1], text_y = lax.optimization_barrier((*ring1, ring2[1], text_y))
    peer1 = [move(v, FLIP_C) for v in ring1]
    text_yc = move(text_y, FLIP_C)
    peer2 = [move(v, FLIP_C) for v in ring2]

    half = 2 * KIND * KIND * WIDTH
    s1, x, st1 = call(
        scores_first,
        (shape(KIND, KIND), mat(2, KIND, WIDTH), shape(8, KIND)),
        [SMEM] * 2 + [VMEM] * 12,
        flops=half,
        bytes_accessed=KIND * KIND * 4,
    )(core, logit_scale, first, *ring1, second, *ring2, peer_first, *peer1)
    s2, y, st = call(
        scores_second,
        (shape(KIND, KIND), mat(2, KIND, WIDTH), shape(8, KIND)),
        [SMEM] * 2 + [VMEM] * 10,
        scratch=[pltpu.VMEM((8, KIND), F32)],
        flops=half,
        bytes_accessed=KIND * KIND * 4,
    )(core, logit_scale, x, st1, image_other, *ring2, text_yc, *peer2)

    stats = shape(8, KIND)
    held = (s1, s2, x, y)
    side = call(join_cores, stats, [SMEM] + [VMEM] * 6)(core, st, move(st, FLIP_C), *held)
    side = call(join_pair, stats, [VMEM] * 6)(side, move(side, FLIP_Y), *held)
    others = [move(side, AHEAD[4 - k]) for k in (1, 2, 3)]
    side = call(join_ring, stats, [VMEM] * 8)(side, *others, *held)
    peer = move(side, FLIP_C)

    weights = lambda kind, s: call(functools.partial(grad_weights, kind), mat(KIND, KIND), [SMEM] + [VMEM] * 3)(
        core, s, side, peer
    )
    g2 = weights(1, s2)
    r2 = move(g2, FLIP_C)
    g1 = weights(0, s1)
    r1 = move(g1, FLIP_C)
    long, own, small = mat(CHIP + EXTRA, WIDTH), shape(CHIP, WIDTH), shape(8, 128)

    def grads(body, out_shape, *operands):
        return call(body, out_shape, [SMEM] + [VMEM] * len(operands), flops=half)(core, *operands)

    send_2, send_3 = grads(functools.partial(grads_other, 1), (long, long), g1, g2, r2, x, y, side, peer)
    acc2, send_1, term = grads(functools.partial(grads_other, 0), (own, long, small), g1, g2, r2, x, y, side, peer)
    got2 = [move(v, AHEAD[k + 1]) for k, v in enumerate((send_1, send_2, send_3))]
    send_2, send_3 = grads(functools.partial(grads_own, 1), (chip, chip), g1, r1, r2, x, y)
    half_chip = mat(PIECE, WIDTH)
    acc1, near_same, near_cross = grads(functools.partial(grads_own, 0), (own, half_chip, half_chip), g1, r1, r2, x, y)
    near_same, near_cross = move(near_same, AHEAD[1]), move(near_cross, AHEAD_CROSS)
    got1 = [move(send_2, AHEAD[2]), move(send_3, AHEAD[3])]
    piece, part, tail = mat(PIECE, WIDTH), mat(PIECE // 2, WIDTH), mat(PIECE + EXTRA, WIDTH)
    same, cross, total = grads(sum_other, (tail, tail, small), acc2, *got2, term, send_2, acc1)
    same, cross = move(same, FLIP_Y), move(cross, CROSS_Y)
    keep, give_a, give_b = grads(
        sum_own, (shape(PIECE, WIDTH), mat(PIECE // 2 + EXTRA, WIDTH), part), acc1, *got1, total
    )
    grad_image, grad_text, loss = call(
        finish, (piece, piece, shape(1)), [SMEM] * 2 + [VMEM] * 8, out_specs=(VMEM, VMEM, SMEM)
    )(core, logit_scale, keep, move(give_a, FLIP_C), move(give_b, FLIP_C), same, cross, near_same, near_cross, total)
    return loss, grad_image, grad_text


def solution(mesh):
    fine = Mesh(mesh.devices.reshape(SIZES), AXES)
    every = P(AXES, None)
    return jax.shard_map(
        on_device,
        mesh=fine,
        in_specs=(P(("x", "z", "yh"), None), every, P()),
        out_specs=(P(), every, every),
        check_vma=False,
    )
```
